128 devices in a mesh: dp: 4 (over y), tp: 32 (over z, x, core).
Axes of the slice: x: 4, y: 4, z: 4, core: 2. Of those that a mesh axis runs over, the one named last changes fastest.
Arguments:
- activations: bfloat16 [16384, 8192], P('dp', 'tp'), may hold values from -6 to 6
- out_grads: bfloat16 [16384, 8192], P('dp'), may hold values from -0.09375 to 0.09375
- residual: bfloat16 [32768, 8192], P(('dp', 'tp')), may hold values from -6 to 6
- query_factor: float32 [8192, 64], replicated, may hold values from -0.0625 to 0.0625
Outputs:
- new_error: bfloat16 [32768, 8192], P(('dp', 'tp'))
- right_new: float32 [8192, 64], replicated
The draws below stay inside these ranges and needn't reach their ends.
All inputs are finite; a program needn't handle non-finite values.
Results may differ from the reference program's by a relative error of at most 0.001.
Values sent between devices are 32-bit elements; how exact they have to be, the bound alone decides.
A program may use at most 192 MiB of HBM per device.

```python
import jax
import jax.numpy as jnp
from jax import lax

D = 8192
R = 64
TOK_REP = 4096
TOKENS = 16384
ROWS_ALL = 32768
N_DP = 4


def level_of(stream_key, extent, split, least, top_value):
    level = 1.0
    for dim, blocks in split:
        draws = jax.random.uniform(jax.random.fold_in(jax.random.fold_in(stream_key, 6), dim), (blocks,), jnp.float32, least / len(split), top_value / len(split))
        level = level * jnp.repeat(jnp.exp(draws), extent[dim] // blocks).reshape((-1,) + (1,) * (len(extent) - 1 - dim))
    return level


def scatter_about(rng, extent, deviation, most, pieces=(), dtype=jnp.bfloat16):
    values = deviation * jax.random.normal(rng, extent, jnp.float32)
    if pieces:
        values = values * level_of(rng, extent, pieces, -0.22, 0.18)
    return jnp.clip(values, -most, most).astype(dtype)


def setup_inputs(seed: int = 0) -> dict:
    splits = jax.random.split(jax.random.key(seed), 5)
    return {
        "activations": scatter_about(splits[0], (TOKENS, D), 1.0, 6.0, ((0, 4), (1, 32))),
        "out_grads": scatter_about(splits[1], (TOKENS, D), (TOK_REP ** -0.5), 0.09375, ((0, 4),)),
        "residual": scatter_about(splits[2], (ROWS_ALL, D), 1.0, 6.0, ((0, 128),)),
        "query_factor": scatter_about(splits[3], (D, R), D ** -0.5, 0.0625, (), jnp.float32),
    }


def reference(activations, out_grads, residual, query_factor):
    highest = lax.Precision.HIGHEST
    mergeds = []
    averaged = jnp.zeros((D, R), jnp.float32)
    for replica in range(N_DP):
        act_rows = activations[replica * TOK_REP:(replica + 1) * TOK_REP]
        grad_rows = out_grads[replica * TOK_REP:(replica + 1) * TOK_REP]
        gradient = jnp.dot(act_rows.T.astype(jnp.float32), grad_rows.astype(jnp.float32), preferred_element_type=jnp.float32)
        merged = gradient + residual[replica * D:(replica + 1) * D].astype(jnp.float32)
        mergeds.append(merged)
        averaged = averaged + jnp.dot(merged, query_factor, precision=highest)
    averaged = averaged / N_DP
    gram_matrix = jnp.dot(averaged.T, averaged, precision=highest)
    cholesky_lower = jnp.linalg.cholesky(gram_matrix)
    orthonormal = lax.linalg.triangular_solve(cholesky_lower, averaged, left_side=False, lower=True, transpose_a=True)
    right_new = jnp.zeros((D, R), jnp.float32)
    for merged in mergeds:
        right_new = right_new + jnp.dot(merged.T, orthonormal, precision=highest)
    right_new = right_new / N_DP
    errors = [(merged - jnp.dot(orthonormal, right_new.T, precision=highest)).astype(jnp.bfloat16) for merged in mergeds]
    return (jnp.concatenate(errors, axis=0), right_new)
```

```python
import functools

import jax
import jax.numpy as jnp
from jax import lax
from jax.experimental import pallas as pl
from jax.experimental.pallas import tpu as pltpu
from jax.sharding import PartitionSpec as P

MESH = pl.DeviceIdType.MESH
F32, BF16 = jnp.float32, jnp.bfloat16
HIGHEST = lax.Precision.HIGHEST
TILE = 1024
GROUPS = 4
AXES = ("x", "z", "y", "x")
PHASES = ("core", "line", "plane", "ag_plane", "ag_line", "ag_core")
N_SEMS = 5 + GROUPS * len(PHASES)


def halves(v):
    high = v.astype(BF16)
    return high, (v - high.astype(F32)).astype(BF16)


def thirds(v):
    high = v.astype(BF16)
    rest = v - high.astype(F32)
    mid = rest.astype(BF16)
    return high, mid, (rest - mid.astype(F32)).astype(BF16)


def dot(a, b, ca, cb, precision=None):
    return lax.dot_general(a, b, (((ca,), (cb,)), ((), ())), precision=precision, preferred_element_type=F32)


def kernel(sizes, act_hbm, grad_hbm, res_hbm, query_hbm, error_hbm, right_hbm,
           act, gbuf, res, query, query3, gslice, merged, gq, left, avg, avg2, gram_in, gram_out, gram_slots, chol,
           wl3, tt, core_rx, line_rx, line_sum, plane_rx, tf, right, send, recv, load, gload, store):
    ny, nz, nx = sizes["y"], sizes["z"], sizes["x"]
    dp, tp = lax.axis_index("dp"), lax.axis_index("tp")
    me = {"y": dp, "z": tp // (2 * nx), "x": (tp // 2) % nx}
    core = tp % 2
    rank, width = query_hbm.shape
    tokens, rows = act_hbm.shape
    n_tiles = width // TILE
    gcols = width // GROUPS
    half = rank // 2

    def device(**to):
        at = {**me, "c": core, **to}
        return (at["y"], (at["z"] * nx + at["x"]) * 2 + at["c"])

    def shift(axis, k):
        return lax.rem(me[axis] + k, sizes[axis])

    partner = device(c=1 - core)
    chip = me["z"] * nx + me["x"]
    n_plane = nz * nx

    def to_plane(b1, b2, act_on):
        n2 = sizes[b2]

        @pl.loop(1, sizes[b1] * n2)
        def _(k):
            p1, p2 = shift(b1, k // n2), shift(b2, k % n2)
            act_on(device(**{b1: p1, b2: p2}), p1 * n2 + p2)

    def to_line(axis, act_on):
        @pl.loop(1, sizes[axis])
        def _(k):
            p = shift(axis, k)
            act_on(device(**{axis: p}), p)

    sent = []

    def remote(src, dst, sem, dev):
        pltpu.make_async_remote_copy(
            src_ref=src, dst_ref=dst, send_sem=send.at[sem], recv_sem=recv.at[sem], device_id=dev, device_id_type=MESH
        ).start()

    def arrived(view, sem):
        pltpu.make_async_copy(view(), view(), recv.at[sem]).wait()
        sent.append((view, sem))

    def at_group(g):
        return pl.ds(gcols * g, gcols)

    def sem_of(g, phase):
        return 5 + g * len(PHASES) + PHASES.index(phase)

    slot = core * n_plane + chip
    slice_rows = tokens // (2 * n_plane)
    loads = [
        pltpu.make_async_copy(query_hbm, query, load.at[0]),
        pltpu.make_async_copy(grad_hbm.at[pl.ds(pl.multiple_of(slot * slice_rows, slice_rows), slice_rows)], gslice, load.at[1]),
        pltpu.make_async_copy(act_hbm, act, load.at[2]),
        pltpu.make_async_copy(res_hbm, res, load.at[3]),
    ]

    def tile_load(i):
        b = lax.rem(i, 2)
        return pltpu.make_async_copy(grad_hbm.at[:, pl.ds(pl.multiple_of(i * TILE, TILE), TILE)], gbuf.at[b], gload.at[b])

    for c in loads[:3]:
        c.start()
    tile_load(0).start()
    loads[3].start()
    tile_load(1).start()

    barrier = pltpu.get_barrier_semaphore()

    def greet(dev, _):
        pl.semaphore_signal(barrier, inc=1, device_id=dev, device_id_type=MESH)

    greet(partner, 0)
    to_plane("z", "x", greet)

    @pl.loop(1, ny)
    def _(k):
        y = shift("y", k)

        @pl.loop(0, nx)
        def _(j):
            greet(device(y=y, x=shift("x", j)), 0)

        @pl.loop(1, nz)
        def _(j):
            greet(device(y=y, z=shift("z", j)), 0)

    n_greet = 1 + n_plane - 1 + (ny - 1) * (nx + nz - 1)

    loads[0].wait()
    loads[1].wait()

    @pl.loop(0, n_tiles)
    def _(i):
        cols = pl.ds(pl.multiple_of(i * TILE, TILE), TILE)
        for j, part in enumerate(thirds(query[:, cols])):
            query3[j * rank:(j + 1) * rank, cols] = part

    def fold3(v):
        return v[:rank] + (v[rank:2 * rank] + v[2 * rank:])

    gq_cols = pl.ds(pl.multiple_of(slot * slice_rows, slice_rows), slice_rows)
    gq[:, gq_cols] = fold3(dot(query3[...], gslice[...], 1, 1))
    pl.semaphore_wait(barrier, n_greet)
    to_plane("z", "x", lambda dev, _: remote(gq.at[:, gq_cols], gq.at[:, gq_cols], 0, dev))

    def tile(i):
        cols = pl.ds(pl.multiple_of(i * TILE, TILE), TILE)
        tile_load(i).wait()
        product = dot(act[...], gbuf[lax.rem(i, 2)], 0, 0)
        merged[:, cols] = product + res[:, cols].astype(F32)

        @pl.when(i + 2 < n_tiles)
        def _():
            tile_load(i + 2).start()

    def gq_core():
        arrived(lambda: gq.at[:, pl.ds(0, (n_plane - 1) * slice_rows)], 0)
        mine = gq.at[:, pl.ds(pl.multiple_of(core * n_plane * slice_rows, slice_rows), n_plane * slice_rows)]
        remote(mine, mine, 1, partner)

    def left_factor():
        arrived(lambda: gq.at[:, pl.ds(0, n_plane * slice_rows)], 1)
        total = fold3(dot(query3[...], res[...], 1, 1))
        total += fold3(dot(jnp.concatenate(thirds(gq[...]), axis=0), act[...], 1, 0))
        left[dp] = total
        to_line("y", lambda dev, _: remote(left.at[dp], left.at[dp], 2, dev))

    def average():
        arrived(lambda: left.at[pl.ds(0, ny - 1)], 2)
        total = left[0]
        for r in range(1, ny):
            total = total + left[r]
        total = total * (1.0 / ny)
        avg[...] = total
        high, low = halves(total)
        avg2[:rank] = high
        avg2[rank:] = low
        gram = dot(total, total, 1, 1, HIGHEST)
        gram_out[...] = jnp.concatenate([gram[:half], gram[half:]], axis=1)
        remote(gram_out, gram_in, 3, partner)

    def gram_sum():
        arrived(lambda: gram_in, 3)
        gram_slots[chip] = gram_out[...] + gram_in[...]
        to_plane("z", "x", lambda dev, _: remote(gram_slots.at[chip], gram_slots.at[chip], 4, dev))

    def right_terms(g):
        step = 512

        @pl.loop(0, gcols // step)
        def _(i):
            cols = pl.ds(pl.multiple_of(gcols * g + i * step, step), step)
            high, low = halves(merged[:, cols])
            both = dot(avg2[...], high, 1, 0)
            tt[:, cols] = both[:rank] + (both[rank:] + dot(avg2[:rank], low, 1, 0))

        theirs = pl.ds(pl.multiple_of(half * (1 - core), half), half)
        remote(tt.at[theirs, at_group(g)], core_rx.at[:, at_group(g)], sem_of(g, "core"), partner)

    def line_of(g):
        axis = AXES[g]
        b1, b2 = [a for a in ("y", "z", "x") if a != axis]
        n = sizes[axis]
        n_p = sizes[b1] * sizes[b2]
        return axis, b1, b2, n, half // n, me[b1] * sizes[b2] + me[b2], n_p, gcols // n_p

    def part_rows(p, size):
        return pl.ds(pl.multiple_of(p * size, size), size)

    def line_send(g):
        axis, _, _, n, lrows, *_ = line_of(g)
        cols = at_group(g)
        arrived(lambda: core_rx.at[:, cols], sem_of(g, "core"))
        core_rx[:, cols] = core_rx[:, cols] + tt[part_rows(core, half), cols]
        to_line(axis, lambda dev, p: remote(
            core_rx.at[part_rows(p, lrows), cols], line_rx.at[g, part_rows(me[axis], lrows)], sem_of(g, "line"), dev))

    def plane_send(g):
        axis, b1, b2, n, lrows, pos, n_p, pcols = line_of(g)
        arrived(lambda: line_rx.at[g, pl.ds(0, (n - 1) * lrows)], sem_of(g, "line"))
        total = core_rx[part_rows(me[axis], lrows), at_group(g)]
        for k in range(1, n):
            total = total + line_rx[g, part_rows(shift(axis, k), lrows)]
        line_sum[g, :lrows] = total
        to_plane(b1, b2, lambda dev, p: remote(
            line_sum.at[g, pl.ds(0, lrows), part_rows(p, pcols)],
            plane_rx.at[g, pl.ds(0, lrows), part_rows(pos, pcols)], sem_of(g, "plane"), dev))

    def gather_plane(g):
        axis, b1, b2, n, lrows, pos, n_p, pcols = line_of(g)
        rest = pl.ds(0, (n_p - 1) * pcols)
        arrived(lambda: plane_rx.at[g, pl.ds(0, lrows), rest], sem_of(g, "plane"))
        mine = part_rows(pos, pcols)
        plane_rx[g, :lrows, mine] = line_sum[g, :lrows, mine]
        total = plane_rx[g, :lrows, 0:pcols]
        for k in range(1, n_p):
            total = total + plane_rx[g, :lrows, k * pcols:(k + 1) * pcols]
        piece = (pl.ds(pl.multiple_of(half * core + lrows * me[axis], lrows), lrows),
                 pl.ds(pl.multiple_of(gcols * g + pcols * pos, pcols), pcols))
        tf[piece] = total
        to_plane(b1, b2, lambda dev, _: remote(tf.at[piece], tf.at[piece], sem_of(g, "ag_plane"), dev))

    def gather_line(g):
        axis, b1, b2, n, lrows, pos, n_p, pcols = line_of(g)
        arrived(lambda: tf.at[pl.ds(0, lrows), pl.ds(0, (n_p - 1) * pcols)], sem_of(g, "ag_plane"))
        piece = (pl.ds(pl.multiple_of(half * core + lrows * me[axis], lrows), lrows), at_group(g))
        to_line(axis, lambda dev, _: remote(tf.at[piece], tf.at[piece], sem_of(g, "ag_line"), dev))

    def gather_core(g):
        axis, b1, b2, n, lrows, *_ = line_of(g)
        arrived(lambda: tf.at[pl.ds(0, (n - 1) * lrows), at_group(g)], sem_of(g, "ag_line"))
        mine = tf.at[part_rows(core, half), at_group(g)]
        remote(mine, mine, sem_of(g, "ag_core"), partner)

    def cholesky():
        arrived(lambda: gram_slots.at[pl.ds(0, n_plane - 1)], 4)
        packed = gram_slots[0]
        for k in range(1, n_plane):
            packed = packed + gram_slots[k]
        gram = jnp.concatenate([packed[:, :rank], packed[:, rank:]], axis=0)
        at_row = lax.broadcasted_iota(jnp.int32, (rank, 1), 0)
        at_lane = lax.broadcasted_iota(jnp.int32, (1, 2 * rank), 1)
        unit = (lax.broadcasted_iota(jnp.int32, (rank, rank), 0) == lax.broadcasted_iota(jnp.int32, (rank, rank), 1)).astype(F32)
        chol[...] = jnp.concatenate([gram, unit], axis=1)

        @pl.loop(0, rank)
        def _(k):
            matrix = chol[...]
            row = chol[pl.ds(k, 1), :]
            column = jnp.sum(jnp.where(at_lane == k, matrix, 0.0), axis=1, keepdims=True)
            pivot = jnp.sum(jnp.where(at_lane == k, row, 0.0), axis=1, keepdims=True)
            scale = 1.0 / jnp.sqrt(pivot)
            row = row * scale
            chol[...] = jnp.where(at_row == k, row, matrix - jnp.where(at_row > k, column * scale, 0.0) * row)

        inverse = chol[:, rank:]
        orth = dot(inverse, avg[...], 1, 0, HIGHEST)
        both = jnp.concatenate([dot(inverse, orth, 0, 0, HIGHEST), inverse.T, jnp.zeros((rank, rank), F32)], axis=1)
        high, low = halves(both * (1.0 / ny))
        wl3[:rank] = high
        wl3[rank:2 * rank] = high
        wl3[2 * rank:] = low

    def out_copies(g):
        return [pltpu.make_async_copy(res.at[:, at_group(g)], error_hbm.at[:, at_group(g)], store.at[g, 0]),
                pltpu.make_async_copy(right.at[:, at_group(g)], right_hbm.at[:, at_group(g)], store.at[g, 1])]

    def finish(g):
        step = 512
        arrived(lambda: tf.at[pl.ds(0, half), at_group(g)], sem_of(g, "ag_core"))

        @pl.loop(0, gcols // step)
        def _(i):
            cols = pl.ds(pl.multiple_of(gcols * g + i * step, step), step)
            high, low = halves(tf[:, cols])
            both = dot(wl3[...], jnp.concatenate([high, low, high], axis=0), 0, 0)
            res[:, cols] = (merged[:, cols] - both[:rows]).astype(BF16)
            right[:, cols] = both[rows:rows + rank]

        for c in out_copies(g):
            c.start()

    loads[2].wait()
    loads[3].wait()
    early = range(GROUPS - 1)
    last = GROUPS - 1

    def after_5():
        average()
        for g in early:
            right_terms(g)

    def after_6():
        gram_sum()
        for g in early:
            line_send(g)

    def after_7():
        right_terms(last)
        for g in early:
            plane_send(g)

    stages = {2: gq_core, 3: left_factor, 5: after_5, 6: after_6, 7: after_7}

    @pl.loop(0, n_tiles)
    def _(i):
        tile(i)
        for at, stage in stages.items():
            pl.when(i == at)(stage)

    line_send(last)
    for g in early:
        gather_plane(g)
    plane_send(last)
    for g in early:
        gather_line(g)
    cholesky()
    gather_plane(last)
    for g in early:
        gather_core(g)
    gather_line(last)
    for g in early:
        finish(g)
    gather_core(last)
    finish(last)
    for g in range(GROUPS):
        for c in out_copies(g):
            c.wait()
    for view, sem in sent:
        pltpu.make_async_copy(view(), view(), send.at[sem]).wait()


def solution(mesh):
    n_dp, n_tp = mesh.shape["dp"], mesh.shape["tp"]
    nx = 4 if n_tp == 32 else 2
    sizes = {"y": n_dp, "z": n_tp // (2 * nx), "x": nx}

    def on_device(activations, out_grads, residual, query_factor):
        tokens, rows = activations.shape
        width, rank = query_factor.shape
        half = rank // 2
        gcols = width // GROUPS
        n_plane = sizes["z"] * sizes["x"]
        lmax = half // min(sizes.values())
        error, right_t = pl.pallas_call(
            functools.partial(kernel, sizes),
            out_shape=(jax.ShapeDtypeStruct((rows, width), BF16), jax.ShapeDtypeStruct((rank, width), F32)),
            in_specs=[pl.BlockSpec(memory_space=pl.ANY)] * 4,
            out_specs=(pl.BlockSpec(memory_space=pl.ANY),) * 2,
            scratch_shapes=[
                pltpu.VMEM((tokens, rows), BF16),
                pltpu.VMEM((2, tokens, TILE), BF16),
                pltpu.VMEM((rows, width), BF16),
                pltpu.VMEM((rank, width), F32),
                pltpu.VMEM((3 * rank, width), BF16),
                pltpu.VMEM((tokens // (2 * n_plane), width), BF16),
                pltpu.VMEM((rows, width), F32),
                pltpu.VMEM((rank, tokens), F32),
                pltpu.VMEM((n_dp, rank, rows), F32),
                pltpu.VMEM((rank, rows), F32),
                pltpu.VMEM((2 * rank, rows), BF16),
                pltpu.VMEM((half, 2 * rank), F32),
                pltpu.VMEM((half, 2 * rank), F32),
                pltpu.VMEM((n_plane, half, 2 * rank), F32),
                pltpu.VMEM((rank, 2 * rank), F32),
                pltpu.VMEM((3 * rank, rows + 2 * rank), BF16),
                pltpu.VMEM((rank, width), F32),
                pltpu.VMEM((half, width), F32),
                pltpu.VMEM((GROUPS, half, gcols), F32),
                pltpu.VMEM((GROUPS, lmax, gcols), F32),
                pltpu.VMEM((GROUPS, lmax, gcols), F32),
                pltpu.VMEM((rank, width), F32),
                pltpu.VMEM((rank, width), F32),
                pltpu.SemaphoreType.DMA((N_SEMS,)),
                pltpu.SemaphoreType.DMA((N_SEMS,)),
                pltpu.SemaphoreType.DMA((4,)),
                pltpu.SemaphoreType.DMA((2,)),
                pltpu.SemaphoreType.DMA((GROUPS, 2)),
            ],
            compiler_params=pltpu.CompilerParams(
                collective_id=0, has_side_effects=True, vmem_limit_bytes=60 * 2**20
            ),
            name="powersgd",
        )(activations, out_grads, residual, query_factor.T)
        return error, right_t.T

    return jax.shard_map(
        on_device,
        mesh=mesh,
        in_specs=(P("dp", "tp"), P("dp", None), P(("dp", "tp"), None), P()),
        out_specs=(P(("dp", "tp"), None), P()),
        check_vma=False,
    )
```

```python
import functools

import jax
import jax.numpy as jnp
from jax import lax
from jax.experimental import pallas as pl
from jax.experimental.pallas import tpu as pltpu
from jax.sharding import PartitionSpec as P

MESH = pl.DeviceIdType.MESH
F32, BF16 = jnp.float32, jnp.bfloat16
HIGHEST = lax.Precision.HIGHEST
TILE = 1024
GROUPS = 4
AXES = ("x", "z", "y")
SLOTS = 3
PHASES = ("core", "line", "plane", "ag_plane", "ag_line", "ag_core")
N_SEMS = 5 + GROUPS * len(PHASES)


def halves(v):
    high = v.astype(BF16)
    return high, (v - high.astype(F32)).astype(BF16)


def thirds(v):
    high = v.astype(BF16)
    rest = v - high.astype(F32)
    mid = rest.astype(BF16)
    return high, mid, (rest - mid.astype(F32)).astype(BF16)


def dot(a, b, ca, cb, precision=None):
    return lax.dot_general(a, b, (((ca,), (cb,)), ((), ())), precision=precision, preferred_element_type=F32)


def kernel(sizes, act_hbm, grad_hbm, res_hbm, query_hbm, res, right,
           act, gbuf, query3, gslice, merged, gq, left, avg, avg2, gram_in, gram_out, gram_slots, chol,
           wl3, tt, core_rx, line_rx, line_sum, plane_rx, last_rx, tf, send, recv, load, gload):
    query = right
    ny, nz, nx = sizes["y"], sizes["z"], sizes["x"]
    dp, tp = lax.axis_index("dp"), lax.axis_index("tp")
    me = {"y": dp, "z": tp // (2 * nx), "x": (tp // 2) % nx}
    core = tp % 2
    rank, width = query_hbm.shape
    tokens, rows = act_hbm.shape
    n_tiles = width // TILE
    gcols = width // GROUPS
    half = rank // 2

    def device(**to):
        at = {**me, "c": core, **to}
        return (at["y"], (at["z"] * nx + at["x"]) * 2 + at["c"])

    def shift(axis, k):
        return lax.rem(me[axis] + k, sizes[axis])

    partner = device(c=1 - core)
    chip = me["z"] * nx + me["x"]
    n_plane = nz * nx
    n_chips = ny * n_plane
    place = dp * n_plane + chip

    def to_plane(b1, b2, act_on):
        n2 = sizes[b2]

        @pl.loop(1, sizes[b1] * n2)
        def _(k):
            p1, p2 = shift(b1, k // n2), shift(b2, k % n2)
            act_on(device(**{b1: p1, b2: p2}), p1 * n2 + p2)

    def to_line(axis, act_on):
        @pl.loop(1, sizes[axis])
        def _(k):
            p = shift(axis, k)
            act_on(device(**{axis: p}), p)

    def to_all(act_on):
        @pl.loop(1, n_chips)
        def _(k):
            y, z, x = shift("y", k // n_plane), shift("z", (k // nx) % nz), shift("x", k % nx)
            act_on(device(y=y, z=z, x=x), (y * nz + z) * nx + x)

    sent = []

    def remote(src, dst, sem, dev):
        pltpu.make_async_remote_copy(
            src_ref=src, dst_ref=dst, send_sem=send.at[sem], recv_sem=recv.at[sem], device_id=dev, device_id_type=MESH
        ).start()

    def arrived(view, sem):
        pltpu.make_async_copy(view(), view(), recv.at[sem]).wait()
        sent.append((view, sem))

    def at_group(g):
        return pl.ds(gcols * g, gcols)

    def sem_of(g, phase):
        return 5 + g * len(PHASES) + PHASES.index(phase)

    slot = core * n_plane + chip
    slice_rows = tokens // (2 * n_plane)
    loads = [
        pltpu.make_async_copy(query_hbm, query, load.at[0]),
        pltpu.make_async_copy(grad_hbm.at[pl.ds(pl.multiple_of(slot * slice_rows, slice_rows), slice_rows)], gslice, load.at[1]),
        pltpu.make_async_copy(res_hbm, res, load.at[2]),
        pltpu.make_async_copy(act_hbm, act, load.at[3]),
    ]

    def tile_load(i):
        b = lax.rem(i, SLOTS)
        return pltpu.make_async_copy(grad_hbm.at[:, pl.ds(pl.multiple_of(i * TILE, TILE), TILE)], gbuf.at[b], gload.at[b])

    for c in loads:
        c.start()
    for b in range(SLOTS):
        tile_load(b).start()

    barrier = pltpu.get_barrier_semaphore()

    def greet(dev, _):
        pl.semaphore_signal(barrier, inc=1, device_id=dev, device_id_type=MESH)

    greet(partner, 0)
    to_all(greet)
    n_greet = 1 + n_chips - 1

    loads[0].wait()
    loads[1].wait()

    def fold3(v):
        return v[:rank] + (v[rank:2 * rank] + v[2 * rank:])

    gq_cols = pl.ds(pl.multiple_of(slot * slice_rows, slice_rows), slice_rows)
    gq[:, gq_cols] = jnp.zeros((rank, slice_rows), F32)

    @pl.loop(0, n_tiles)
    def _(i):
        cols = pl.ds(pl.multiple_of(i * TILE, TILE), TILE)
        parts = jnp.concatenate(thirds(query[:, cols]), axis=0)
        query3[:, cols] = parts
        gq[:, gq_cols] += fold3(dot(parts, gslice[:, cols], 1, 1))

    pl.semaphore_wait(barrier, n_greet)
    to_plane("z", "x", lambda dev, _: remote(gq.at[:, gq_cols], gq.at[:, gq_cols], 0, dev))

    loads[2].wait()
    left[dp] = jnp.zeros((rank, rows), F32)

    @pl.loop(0, n_tiles)
    def _(i):
        cols = pl.ds(pl.multiple_of(i * TILE, TILE), TILE)
        left[dp] += fold3(dot(query3[:, cols], res[:, cols], 1, 1))

    loads[3].wait()

    def tile(i):
        cols = pl.ds(pl.multiple_of(i * TILE, TILE), TILE)
        tile_load(i).wait()
        product = dot(act[...], gbuf[lax.rem(i, SLOTS)], 0, 0)
        merged[:, cols] = product + res[:, cols].astype(F32)

        @pl.when(i + SLOTS < n_tiles)
        def _():
            tile_load(i + SLOTS).start()

    def gq_core():
        arrived(lambda: gq.at[:, pl.ds(0, (n_plane - 1) * slice_rows)], 0)
        mine = gq.at[:, pl.ds(pl.multiple_of(core * n_plane * slice_rows, slice_rows), n_plane * slice_rows)]
        remote(mine, mine, 1, partner)

    def left_factor():
        arrived(lambda: gq.at[:, pl.ds(0, n_plane * slice_rows)], 1)
        step = tokens // 4

        @pl.loop(0, 4)
        def _(i):
            part = pl.ds(pl.multiple_of(i * step, step), step)
            left[dp] += fold3(dot(jnp.concatenate(thirds(gq[:, part]), axis=0), act[part, :], 1, 0))

        to_line("y", lambda dev, _: remote(left.at[dp], left.at[dp], 2, dev))

    def average():
        arrived(lambda: left.at[pl.ds(0, ny - 1)], 2)
        total = left[0]
        for r in range(1, ny):
            total = total + left[r]
        total = total * (1.0 / ny)
        avg[...] = total
        high, low = halves(total)
        avg2[:rank] = high
        avg2[rank:] = low
        gram = dot(total, total, 1, 1, HIGHEST)
        gram_out[...] = jnp.concatenate([gram[:half], gram[half:]], axis=1)
        remote(gram_out, gram_in, 3, partner)

    def gram_sum():
        arrived(lambda: gram_in, 3)
        gram_slots[chip] = gram_out[...] + gram_in[...]
        to_plane("z", "x", lambda dev, _: remote(gram_slots.at[chip], gram_slots.at[chip], 4, dev))

    def right_terms(groups):
        step = 512

        @pl.loop(groups[0] * gcols // step, (groups[-1] + 1) * gcols // step)
        def _(i):
            cols = pl.ds(pl.multiple_of(i * step, step), step)
            high, low = halves(merged[:, cols])
            both = dot(avg2[...], high, 1, 0)
            tt[:, cols] = both[:rank] + (both[rank:] + dot(avg2[:rank], low, 1, 0))

        theirs = pl.ds(pl.multiple_of(half * (1 - core), half), half)
        for g in groups:
            remote(tt.at[theirs, at_group(g)], core_rx.at[:, at_group(g)], sem_of(g, "core"), partner)

    def line_of(g):
        axis = AXES[g]
        b1, b2 = [a for a in ("y", "z", "x") if a != axis]
        n = sizes[axis]
        n_p = sizes[b1] * sizes[b2]
        return axis, b1, b2, n, half // n, me[b1] * sizes[b2] + me[b2], n_p, gcols // n_p

    def part_rows(p, size):
        return pl.ds(pl.multiple_of(p * size, size), size)

    def core_sum(g):
        cols = at_group(g)
        arrived(lambda: core_rx.at[:, cols], sem_of(g, "core"))
        core_rx[:, cols] = core_rx[:, cols] + tt[part_rows(core, half), cols]
        return cols

    n_col = gcols // 128
    l_group = GROUPS - 1
    l_rows = half * gcols // (128 * n_chips)

    def last_piece(at, top):
        return (pl.ds(pl.multiple_of(top + at // n_col * l_rows, l_rows), l_rows),
                pl.ds(pl.multiple_of(gcols * l_group + at % n_col * 128, 128), 128))

    def last_send():
        core_sum(l_group)
        to_all(lambda dev, p: remote(
            core_rx.at[last_piece(p, 0)], last_rx.at[:, part_rows(place, 128)], sem_of(l_group, "line"), dev))

    def last_gather():
        arrived(lambda: last_rx.at[:, pl.ds(0, (n_chips - 1) * 128)], sem_of(l_group, "line"))
        last_rx[:, part_rows(place, 128)] = core_rx[last_piece(place, 0)]
        total = last_rx[:, 0:128]
        for k in range(1, n_chips):
            total = total + last_rx[:, k * 128:(k + 1) * 128]
        piece = last_piece(place, half * core)
        tf[piece] = total
        to_all(lambda dev, _: remote(tf.at[piece], tf.at[piece], sem_of(l_group, "ag_line"), dev))

    def last_core():
        arrived(lambda: tf.at[pl.ds(0, l_rows), pl.ds(0, (n_chips - 1) * 128)], sem_of(l_group, "ag_line"))
        mine = tf.at[part_rows(core, half), at_group(l_group)]
        remote(mine, mine, sem_of(l_group, "ag_core"), partner)

    def line_send(g):
        axis, _, _, n, lrows, *_ = line_of(g)
        cols = core_sum(g)
        to_line(axis, lambda dev, p: remote(
            core_rx.at[part_rows(p, lrows), cols], line_rx.at[g, part_rows(me[axis], lrows)], sem_of(g, "line"), dev))

    def plane_send(g):
        axis, b1, b2, n, lrows, pos, n_p, pcols = line_of(g)
        arrived(lambda: line_rx.at[g, pl.ds(0, (n - 1) * lrows)], sem_of(g, "line"))
        total = core_rx[part_rows(me[axis], lrows), at_group(g)]
        for k in range(1, n):
            total = total + line_rx[g, part_rows(shift(axis, k), lrows)]
        line_sum[g, :lrows] = total
        to_plane(b1, b2, lambda dev, p: remote(
            line_sum.at[g, pl.ds(0, lrows), part_rows(p, pcols)],
            plane_rx.at[g, pl.ds(0, lrows), part_rows(pos, pcols)], sem_of(g, "plane"), dev))

    def gather_plane(g):
        axis, b1, b2, n, lrows, pos, n_p, pcols = line_of(g)
        rest = pl.ds(0, (n_p - 1) * pcols)
        arrived(lambda: plane_rx.at[g, pl.ds(0, lrows), rest], sem_of(g, "plane"))
        mine = part_rows(pos, pcols)
        plane_rx[g, :lrows, mine] = line_sum[g, :lrows, mine]
        total = plane_rx[g, :lrows, 0:pcols]
        for k in range(1, n_p):
            total = total + plane_rx[g, :lrows, k * pcols:(k + 1) * pcols]
        piece = (pl.ds(pl.multiple_of(half * core + lrows * me[axis], lrows), lrows),
                 pl.ds(pl.multiple_of(gcols * g + pcols * pos, pcols), pcols))
        tf[piece] = total
        to_plane(b1, b2, lambda dev, _: remote(tf.at[piece], tf.at[piece], sem_of(g, "ag_plane"), dev))

    def gather_line(g):
        axis, b1, b2, n, lrows, pos, n_p, pcols = line_of(g)
        arrived(lambda: tf.at[pl.ds(0, lrows), pl.ds(0, (n_p - 1) * pcols)], sem_of(g, "ag_plane"))
        piece = (pl.ds(pl.multiple_of(half * core + lrows * me[axis], lrows), lrows), at_group(g))
        to_line(axis, lambda dev, _: remote(tf.at[piece], tf.at[piece], sem_of(g, "ag_line"), dev))

    def gather_core(g):
        axis, b1, b2, n, lrows, *_ = line_of(g)
        arrived(lambda: tf.at[pl.ds(0, (n - 1) * lrows), at_group(g)], sem_of(g, "ag_line"))
        mine = tf.at[part_rows(core, half), at_group(g)]
        remote(mine, mine, sem_of(g, "ag_core"), partner)

    def cholesky():
        arrived(lambda: gram_slots.at[pl.ds(0, n_plane - 1)], 4)
        packed = gram_slots[0]
        for k in range(1, n_plane):
            packed = packed + gram_slots[k]
        gram = jnp.concatenate([packed[:, :rank], packed[:, rank:]], axis=0)
        at_row = lax.broadcasted_iota(jnp.int32, (rank, 1), 0)
        at_lane = lax.broadcasted_iota(jnp.int32, (1, 2 * rank), 1)
        unit = (lax.broadcasted_iota(jnp.int32, (rank, rank), 0) == lax.broadcasted_iota(jnp.int32, (rank, rank), 1)).astype(F32)
        chol[...] = jnp.concatenate([gram, unit], axis=1)

        @pl.loop(0, rank)
        def _(k):
            matrix = chol[...]
            row = chol[pl.ds(k, 1), :]
            column = jnp.sum(jnp.where(at_lane == k, matrix, 0.0), axis=1, keepdims=True)
            pivot = jnp.sum(jnp.where(at_lane == k, row, 0.0), axis=1, keepdims=True)
            scale = 1.0 / jnp.sqrt(pivot)
            row = row * scale
            chol[...] = jnp.where(at_row == k, row, matrix - jnp.where(at_row > k, column * scale, 0.0) * row)

        inverse = chol[:, rank:]
        orth = dot(inverse, avg[...], 1, 0, HIGHEST)
        both = jnp.concatenate([dot(inverse, orth, 0, 0, HIGHEST), inverse.T, jnp.zeros((rank, rank), F32)], axis=1)
        high, low = halves(both * (1.0 / ny))
        wl3[:rank] = high
        wl3[rank:2 * rank] = high
        wl3[2 * rank:] = low

    def finish(groups):
        step = 512
        for g in groups:
            arrived(lambda g=g: tf.at[pl.ds(0, half), at_group(g)], sem_of(g, "ag_core"))

        @pl.loop(groups[0] * gcols // step, (groups[-1] + 1) * gcols // step)
        def _(i):
            cols = pl.ds(pl.multiple_of(i * step, step), step)
            high, low = halves(tf[:, cols])
            both = dot(wl3[...], jnp.concatenate([high, low, high], axis=0), 0, 0)
            res[:, cols] = (merged[:, cols] - both[:rows]).astype(BF16)
            right[:, cols] = both[rows:rows + rank]

    early = list(range(l_group))

    def after_5():
        average()
        right_terms(early)
        gram_sum()
        for g in early:
            line_send(g)

    stages = {2: gq_core, 3: left_factor, 5: after_5}

    @pl.loop(0, n_tiles)
    def _(i):
        tile(i)
        for at, stage in stages.items():
            pl.when(i == at)(stage)

    right_terms([l_group])
    last_send()
    for g in early:
        plane_send(g)
    cholesky()
    for g in early:
        gather_plane(g)
    last_gather()
    for g in early:
        gather_line(g)
    last_core()
    for g in early:
        gather_core(g)
    finish([l_group])
    finish(early)
    for view, sem in sent:
        pltpu.make_async_copy(view(), view(), send.at[sem]).wait()


def solution(mesh):
    n_dp, n_tp = mesh.shape["dp"], mesh.shape["tp"]
    nx = 4 if n_tp == 32 else 2
    sizes = {"y": n_dp, "z": n_tp // (2 * nx), "x": nx}

    def on_device(activations, out_grads, residual, query_factor):
        tokens, rows = activations.shape
        width, rank = query_factor.shape
        half = rank // 2
        gcols = width // GROUPS
        n_plane = sizes["z"] * sizes["x"]
        lmax = half // min(sizes.values())
        error, right_t = pl.pallas_call(
            functools.partial(kernel, sizes),
            out_shape=(pltpu.VMEM((rows, width), BF16), pltpu.VMEM((rank, width), F32)),
            in_specs=[pl.BlockSpec(memory_space=pl.ANY)] * 4,
            out_specs=(pl.BlockSpec(memory_space=pltpu.VMEM),) * 2,
            scratch_shapes=[
                pltpu.VMEM((tokens, rows), BF16),
                pltpu.VMEM((SLOTS, tokens, TILE), BF16),
                pltpu.VMEM((3 * rank, width), BF16),
                pltpu.VMEM((tokens // (2 * n_plane), width), BF16),
                pltpu.VMEM((rows, width), F32),
                pltpu.VMEM((rank, tokens), F32),
                pltpu.VMEM((n_dp, rank, rows), F32),
                pltpu.VMEM((rank, rows), F32),
                pltpu.VMEM((2 * rank, rows), BF16),
                pltpu.VMEM((half, 2 * rank), F32),
                pltpu.VMEM((half, 2 * rank), F32),
                pltpu.VMEM((n_plane, half, 2 * rank), F32),
                pltpu.VMEM((rank, 2 * rank), F32),
                pltpu.VMEM((3 * rank, rows + 2 * rank), BF16),
                pltpu.VMEM((rank, width), F32),
                pltpu.VMEM((half, width), F32),
                pltpu.VMEM((GROUPS, half, gcols), F32),
                pltpu.VMEM((GROUPS, lmax, gcols), F32),
                pltpu.VMEM((GROUPS, lmax, gcols), F32),
                pltpu.VMEM((half * gcols // (128 * sizes["y"] * n_plane), sizes["y"] * n_plane * 128), F32),
                pltpu.VMEM((rank, width), F32),
                pltpu.SemaphoreType.DMA((N_SEMS,)),
                pltpu.SemaphoreType.DMA((N_SEMS,)),
                pltpu.SemaphoreType.DMA((4,)),
                pltpu.SemaphoreType.DMA((SLOTS,)),
            ],
            compiler_params=pltpu.CompilerParams(
                collective_id=0, has_side_effects=True, vmem_limit_bytes=52 * 2**20
            ),
            name="powersgd",
        )(activations, out_grads, residual, query_factor.T)
        return error, right_t.T

    return jax.shard_map(
        on_device,
        mesh=mesh,
        in_specs=(P("dp", "tp"), P("dp", None), P(("dp", "tp"), None), P()),
        out_specs=(P(("dp", "tp"), None), P()),
        check_vma=False,
    )
```

```python
import functools

import jax
import jax.numpy as jnp
from jax import lax
from jax.experimental import pallas as pl
from jax.experimental.pallas import tpu as pltpu
from jax.sharding import PartitionSpec as P

MESH = pl.DeviceIdType.MESH
F32, BF16 = jnp.float32, jnp.bfloat16
HIGHEST = lax.Precision.HIGHEST
TILE = 1024
GROUPS = 4
AXES = ("x", "z", "y")
SLOTS = 3
PHASES = ("core", "line", "plane", "ag_plane", "ag_line", "ag_core")
N_SEMS = 5 + GROUPS * len(PHASES)


def halves(v):
    high = v.astype(BF16)
    return high, (v - high.astype(F32)).astype(BF16)


def thirds(v):
    high = v.astype(BF16)
    rest = v - high.astype(F32)
    mid = rest.astype(BF16)
    return high, mid, (rest - mid.astype(F32)).astype(BF16)


def dot(a, b, ca, cb, precision=None):
    return lax.dot_general(a, b, (((ca,), (cb,)), ((), ())), precision=precision, preferred_element_type=F32)


def kernel(sizes, act_hbm, grad_hbm, res_hbm, query_hbm, res, right,
           act, gbuf, query3, gslice, merged, gq, left, avg, avg2, gram_in, gram_out, gram_slots, chol,
           wl3, tt, core_rx, line_rx, line_sum, plane_rx, last_rx, tf, send, recv, load, gload):
    query = right
    ny, nz, nx = sizes["y"], sizes["z"], sizes["x"]
    dp, tp = lax.axis_index("dp"), lax.axis_index("tp")
    me = {"y": dp, "z": tp // (2 * nx), "x": (tp // 2) % nx}
    core = tp % 2
    rank, width = query_hbm.shape
    tokens, rows = act_hbm.shape
    n_tiles = width // TILE
    gcols = width // GROUPS
    half = rank // 2

    def device(**to):
        at = {**me, "c": core, **to}
        return (at["y"], (at["z"] * nx + at["x"]) * 2 + at["c"])

    def shift(axis, k):
        return lax.rem(me[axis] + k, sizes[axis])

    partner = device(c=1 - core)
    chip = me["z"] * nx + me["x"]
    n_plane = nz * nx
    n_chips = ny * n_plane
    place = dp * n_plane + chip

    def to_plane(b1, b2, act_on):
        n2 = sizes[b2]

        @pl.loop(1, sizes[b1] * n2)
        def _(k):
            p1, p2 = shift(b1, k // n2), shift(b2, k % n2)
            act_on(device(**{b1: p1, b2: p2}), p1 * n2 + p2)

    def to_line(axis, act_on):
        @pl.loop(1, sizes[axis])
        def _(k):
            p = shift(axis, k)
            act_on(device(**{axis: p}), p)

    def to_all(act_on):
        @pl.loop(1, n_chips)
        def _(k):
            y, z, x = shift("y", k // n_plane), shift("z", (k // nx) % nz), shift("x", k % nx)
            act_on(device(y=y, z=z, x=x), (y * nz + z) * nx + x)

    sent = []

    def remote(src, dst, sem, dev):
        pltpu.make_async_remote_copy(
            src_ref=src, dst_ref=dst, send_sem=send.at[sem], recv_sem=recv.at[sem], device_id=dev, device_id_type=MESH
        ).start()

    def arrived(view, sem):
        pltpu.make_async_copy(view(), view(), recv.at[sem]).wait()
        sent.append((view, sem))

    def at_group(g):
        return pl.ds(gcols * g, gcols)

    def sem_of(g, phase):
        return 5 + g * len(PHASES) + PHASES.index(phase)

    slot = core * n_plane + chip
    slice_rows = tokens // (2 * n_plane)
    loads = [
        pltpu.make_async_copy(query_hbm, query, load.at[0]),
        pltpu.make_async_copy(grad_hbm.at[pl.ds(pl.multiple_of(slot * slice_rows, slice_rows), slice_rows)], gslice, load.at[1]),
        pltpu.make_async_copy(res_hbm, res, load.at[2]),
        pltpu.make_async_copy(act_hbm, act, load.at[3]),
    ]

    def first_load(j):
        cols = pl.ds(pl.multiple_of(j * (TILE // 2), TILE // 2), TILE // 2)
        return pltpu.make_async_copy(grad_hbm.at[:, cols], gbuf.at[0, :, cols], gload.at[SLOTS + j])

    def tile_load(i):
        b = lax.rem(i, SLOTS)
        return pltpu.make_async_copy(grad_hbm.at[:, pl.ds(pl.multiple_of(i * TILE, TILE), TILE)], gbuf.at[b], gload.at[b])

    for c in loads:
        c.start()
    for j in range(2):
        first_load(j).start()
    for b in range(1, SLOTS):
        tile_load(b).start()

    barrier = pltpu.get_barrier_semaphore()

    def greet(dev, _):
        pl.semaphore_signal(barrier, inc=1, device_id=dev, device_id_type=MESH)

    greet(partner, 0)
    to_all(greet)
    n_greet = 1 + n_chips - 1

    loads[0].wait()
    loads[1].wait()

    def fold3(v):
        return v[:rank] + (v[rank:2 * rank] + v[2 * rank:])

    gq_cols = pl.ds(pl.multiple_of(slot * slice_rows, slice_rows), slice_rows)
    gq[:, gq_cols] = jnp.zeros((rank, slice_rows), F32)

    @pl.loop(0, n_tiles)
    def _(i):
        cols = pl.ds(pl.multiple_of(i * TILE, TILE), TILE)
        parts = jnp.concatenate(thirds(query[:, cols]), axis=0)
        query3[:, cols] = parts
        gq[:, gq_cols] += fold3(dot(parts, gslice[:, cols], 1, 1))

    pl.semaphore_wait(barrier, n_greet)
    to_plane("z", "x", lambda dev, _: remote(gq.at[:, gq_cols], gq.at[:, gq_cols], 0, dev))

    loads[2].wait()
    left[dp] = jnp.zeros((rank, rows), F32)

    @pl.loop(0, n_tiles)
    def _(i):
        cols = pl.ds(pl.multiple_of(i * TILE, TILE), TILE)
        left[dp] += fold3(dot(query3[:, cols], res[:, cols], 1, 1))

    loads[3].wait()

    @pl.loop(0, 2)
    def _(j):
        cols = pl.ds(pl.multiple_of(j * (TILE // 2), TILE // 2), TILE // 2)
        first_load(j).wait()
        merged[:, cols] = dot(act[...], gbuf[0, :, cols], 0, 0) + res[:, cols].astype(F32)

    tile_load(SLOTS).start()

    def tile(i):
        cols = pl.ds(pl.multiple_of(i * TILE, TILE), TILE)
        tile_load(i).wait()
        product = dot(act[...], gbuf[lax.rem(i, SLOTS)], 0, 0)
        merged[:, cols] = product + res[:, cols].astype(F32)

        @pl.when(i + SLOTS < n_tiles)
        def _():
            tile_load(i + SLOTS).start()

    def gq_core():
        arrived(lambda: gq.at[:, pl.ds(0, (n_plane - 1) * slice_rows)], 0)
        mine = gq.at[:, pl.ds(pl.multiple_of(core * n_plane * slice_rows, slice_rows), n_plane * slice_rows)]
        remote(mine, mine, 1, partner)

    def left_factor():
        arrived(lambda: gq.at[:, pl.ds(0, n_plane * slice_rows)], 1)
        step = tokens // 4

        @pl.loop(0, 4)
        def _(i):
            part = pl.ds(pl.multiple_of(i * step, step), step)
            left[dp] += fold3(dot(jnp.concatenate(thirds(gq[:, part]), axis=0), act[part, :], 1, 0))

        to_line("y", lambda dev, _: remote(left.at[dp], left.at[dp], 2, dev))

    def average():
        arrived(lambda: left.at[pl.ds(0, ny - 1)], 2)
        total = left[0]
        for r in range(1, ny):
            total = total + left[r]
        total = total * (1.0 / ny)
        avg[...] = total
        high, low = halves(total)
        avg2[:rank] = high
        avg2[rank:] = low
        gram = dot(total, total, 1, 1, HIGHEST)
        gram_out[...] = jnp.concatenate([gram[:half], gram[half:]], axis=1)
        remote(gram_out, gram_in, 3, partner)

    def gram_sum():
        arrived(lambda: gram_in, 3)
        gram_slots[chip] = gram_out[...] + gram_in[...]
        to_plane("z", "x", lambda dev, _: remote(gram_slots.at[chip], gram_slots.at[chip], 4, dev))

    def right_terms(groups):
        step = 512

        @pl.loop(groups[0] * gcols // step, (groups[-1] + 1) * gcols // step)
        def _(i):
            cols = pl.ds(pl.multiple_of(i * step, step), step)
            high, low = halves(merged[:, cols])
            both = dot(avg2[...], high, 1, 0)
            tt[:, cols] = both[:rank] + (both[rank:] + dot(avg2[:rank], low, 1, 0))

        theirs = pl.ds(pl.multiple_of(half * (1 - core), half), half)
        for g in groups:
            remote(tt.at[theirs, at_group(g)], core_rx.at[:, at_group(g)], sem_of(g, "core"), partner)

    def line_of(g):
        axis = AXES[g]
        b1, b2 = [a for a in ("y", "z", "x") if a != axis]
        n = sizes[axis]
        n_p = sizes[b1] * sizes[b2]
        return axis, b1, b2, n, half // n, me[b1] * sizes[b2] + me[b2], n_p, gcols // n_p

    def part_rows(p, size):
        return pl.ds(pl.multiple_of(p * size, size), size)

    def core_sum(g):
        cols = at_group(g)
        arrived(lambda: core_rx.at[:, cols], sem_of(g, "core"))
        core_rx[:, cols] = core_rx[:, cols] + tt[part_rows(core, half), cols]
        return cols

    n_col = gcols // 128
    l_group = GROUPS - 1
    l_rows = half * gcols // (128 * n_chips)

    def last_piece(at, top):
        return (pl.ds(pl.multiple_of(top + at // n_col * l_rows, l_rows), l_rows),
                pl.ds(pl.multiple_of(gcols * l_group + at % n_col * 128, 128), 128))

    def last_send():
        core_sum(l_group)
        to_all(lambda dev, p: remote(
            core_rx.at[last_piece(p, 0)], last_rx.at[:, part_rows(place, 128)], sem_of(l_group, "line"), dev))

    def last_gather():
        arrived(lambda: last_rx.at[:, pl.ds(0, (n_chips - 1) * 128)], sem_of(l_group, "line"))
        last_rx[:, part_rows(place, 128)] = core_rx[last_piece(place, 0)]
        total = last_rx[:, 0:128]
        for k in range(1, n_chips):
            total = total + last_rx[:, k * 128:(k + 1) * 128]
        piece = last_piece(place, half * core)
        tf[piece] = total
        to_all(lambda dev, _: remote(tf.at[piece], tf.at[piece], sem_of(l_group, "ag_line"), dev))

    def last_core():
        arrived(lambda: tf.at[pl.ds(0, l_rows), pl.ds(0, (n_chips - 1) * 128)], sem_of(l_group, "ag_line"))
        mine = tf.at[part_rows(core, half), at_group(l_group)]
        remote(mine, mine, sem_of(l_group, "ag_core"), partner)

    def line_send(g):
        axis, _, _, n, lrows, *_ = line_of(g)
        cols = core_sum(g)
        to_line(axis, lambda dev, p: remote(
            core_rx.at[part_rows(p, lrows), cols], line_rx.at[g, part_rows(me[axis], lrows)], sem_of(g, "line"), dev))

    def plane_send(g):
        axis, b1, b2, n, lrows, pos, n_p, pcols = line_of(g)
        arrived(lambda: line_rx.at[g, pl.ds(0, (n - 1) * lrows)], sem_of(g, "line"))
        total = core_rx[part_rows(me[axis], lrows), at_group(g)]
        for k in range(1, n):
            total = total + line_rx[g, part_rows(shift(axis, k), lrows)]
        line_sum[g, :lrows] = total
        to_plane(b1, b2, lambda dev, p: remote(
            line_sum.at[g, pl.ds(0, lrows), part_rows(p, pcols)],
            plane_rx.at[g, pl.ds(0, lrows), part_rows(pos, pcols)], sem_of(g, "plane"), dev))

    def gather_plane(g):
        axis, b1, b2, n, lrows, pos, n_p, pcols = line_of(g)
        rest = pl.ds(0, (n_p - 1) * pcols)
        arrived(lambda: plane_rx.at[g, pl.ds(0, lrows), rest], sem_of(g, "plane"))
        mine = part_rows(pos, pcols)
        plane_rx[g, :lrows, mine] = line_sum[g, :lrows, mine]
        total = plane_rx[g, :lrows, 0:pcols]
        for k in range(1, n_p):
            total = total + plane_rx[g, :lrows, k * pcols:(k + 1) * pcols]
        piece = (pl.ds(pl.multiple_of(half * core + lrows * me[axis], lrows), lrows),
                 pl.ds(pl.multiple_of(gcols * g + pcols * pos, pcols), pcols))
        tf[piece] = total
        to_plane(b1, b2, lambda dev, _: remote(tf.at[piece], tf.at[piece], sem_of(g, "ag_plane"), dev))

    def gather_line(g):
        axis, b1, b2, n, lrows, pos, n_p, pcols = line_of(g)
        arrived(lambda: tf.at[pl.ds(0, lrows), pl.ds(0, (n_p - 1) * pcols)], sem_of(g, "ag_plane"))
        piece = (pl.ds(pl.multiple_of(half * core + lrows * me[axis], lrows), lrows), at_group(g))
        to_line(axis, lambda dev, _: remote(tf.at[piece], tf.at[piece], sem_of(g, "ag_line"), dev))

    def gather_core(g):
        axis, b1, b2, n, lrows, *_ = line_of(g)
        arrived(lambda: tf.at[pl.ds(0, (n - 1) * lrows), at_group(g)], sem_of(g, "ag_line"))
        mine = tf.at[part_rows(core, half), at_group(g)]
        remote(mine, mine, sem_of(g, "ag_core"), partner)

    def cholesky():
        arrived(lambda: gram_slots.at[pl.ds(0, n_plane - 1)], 4)
        packed = gram_slots[0]
        for k in range(1, n_plane):
            packed = packed + gram_slots[k]
        gram = jnp.concatenate([packed[:, :rank], packed[:, rank:]], axis=0)
        at_row = lax.broadcasted_iota(jnp.int32, (rank, 1), 0)
        at_lane = lax.broadcasted_iota(jnp.int32, (1, 2 * rank), 1)
        unit = (lax.broadcasted_iota(jnp.int32, (rank, rank), 0) == lax.broadcasted_iota(jnp.int32, (rank, rank), 1)).astype(F32)
        chol[...] = jnp.concatenate([gram, unit], axis=1)

        @pl.loop(0, rank)
        def _(k):
            matrix = chol[...]
            row = chol[pl.ds(k, 1), :]
            column = jnp.sum(jnp.where(at_lane == k, matrix, 0.0), axis=1, keepdims=True)
            pivot = jnp.sum(jnp.where(at_lane == k, row, 0.0), axis=1, keepdims=True)
            scale = 1.0 / jnp.sqrt(pivot)
            row = row * scale
            chol[...] = jnp.where(at_row == k, row, matrix - jnp.where(at_row > k, column * scale, 0.0) * row)

        inverse = chol[:, rank:]
        orth = dot(inverse, avg[...], 1, 0, HIGHEST)
        both = jnp.concatenate([dot(inverse, orth, 0, 0, HIGHEST), inverse.T, jnp.zeros((rank, rank), F32)], axis=1)
        high, low = halves(both * (1.0 / ny))
        wl3[:rank] = high
        wl3[rank:2 * rank] = high
        wl3[2 * rank:] = low

    def finish(g):
        step = 512
        arrived(lambda: tf.at[pl.ds(0, half), at_group(g)], sem_of(g, "ag_core"))

        @pl.loop(g * gcols // step, (g + 1) * gcols // step)
        def _(i):
            cols = pl.ds(pl.multiple_of(i * step, step), step)
            high, low = halves(tf[:, cols])
            both = dot(wl3[...], jnp.concatenate([high, low, high], axis=0), 0, 0)
            res[:, cols] = (merged[:, cols] - both[:rows]).astype(BF16)
            right[:, cols] = both[rows:rows + rank]

    early = list(range(l_group))

    def after_5():
        average()
        right_terms(early)

    def after_6():
        gram_sum()
        for g in early:
            line_send(g)

    stages = {2: gq_core, 3: left_factor, 5: after_5, 6: after_6}

    @pl.loop(1, n_tiles)
    def _(i):
        tile(i)
        for at, stage in stages.items():
            pl.when(i == at)(stage)

    right_terms([l_group])
    last_send()
    for g in early:
        plane_send(g)
    cholesky()
    for g in early:
        gather_plane(g)
    last_gather()
    for g in early:
        gather_line(g)
    last_core()
    for g in early:
        gather_core(g)
    for g in [l_group] + early:
        finish(g)
    for view, sem in sent:
        pltpu.make_async_copy(view(), view(), send.at[sem]).wait()


def solution(mesh):
    n_dp, n_tp = mesh.shape["dp"], mesh.shape["tp"]
    nx = 4 if n_tp == 32 else 2
    sizes = {"y": n_dp, "z": n_tp // (2 * nx), "x": nx}

    def on_device(activations, out_grads, residual, query_factor):
        tokens, rows = activations.shape
        width, rank = query_factor.shape
        half = rank // 2
        gcols = width // GROUPS
        n_plane = sizes["z"] * sizes["x"]
        lmax = half // min(sizes.values())
        error, right_t = pl.pallas_call(
            functools.partial(kernel, sizes),
            out_shape=(pltpu.VMEM((rows, width), BF16), pltpu.VMEM((rank, width), F32)),
            in_specs=[pl.BlockSpec(memory_space=pl.ANY)] * 4,
            out_specs=(pl.BlockSpec(memory_space=pltpu.VMEM),) * 2,
            scratch_shapes=[
                pltpu.VMEM((tokens, rows), BF16),
                pltpu.VMEM((SLOTS, tokens, TILE), BF16),
                pltpu.VMEM((3 * rank, width), BF16),
                pltpu.VMEM((tokens // (2 * n_plane), width), BF16),
                pltpu.VMEM((rows, width), F32),
                pltpu.VMEM((rank, tokens), F32),
                pltpu.VMEM((n_dp, rank, rows), F32),
                pltpu.VMEM((rank, rows), F32),
                pltpu.VMEM((2 * rank, rows), BF16),
                pltpu.VMEM((half, 2 * rank), F32),
                pltpu.VMEM((half, 2 * rank), F32),
                pltpu.VMEM((n_plane, half, 2 * rank), F32),
                pltpu.VMEM((rank, 2 * rank), F32),
                pltpu.VMEM((3 * rank, rows + 2 * rank), BF16),
                pltpu.VMEM((rank, width), F32),
                pltpu.VMEM((half, width), F32),
                pltpu.VMEM((GROUPS, half, gcols), F32),
                pltpu.VMEM((GROUPS, lmax, gcols), F32),
                pltpu.VMEM((GROUPS, lmax, gcols), F32),
                pltpu.VMEM((half * gcols // (128 * sizes["y"] * n_plane), sizes["y"] * n_plane * 128), F32),
                pltpu.VMEM((rank, width), F32),
                pltpu.SemaphoreType.DMA((N_SEMS,)),
                pltpu.SemaphoreType.DMA((N_SEMS,)),
                pltpu.SemaphoreType.DMA((4,)),
                pltpu.SemaphoreType.DMA((SLOTS + 2,)),
            ],
            compiler_params=pltpu.CompilerParams(
                collective_id=0, has_side_effects=True, vmem_limit_bytes=52 * 2**20
            ),
            name="powersgd",
        )(activations, out_grads, residual, query_factor.T)
        return error, right_t.T

    return jax.shard_map(
        on_device,
        mesh=mesh,
        in_specs=(P("dp", "tp"), P("dp", None), P(("dp", "tp"), None), P()),
        out_specs=(P(("dp", "tp"), None), P()),
        check_vma=False,
    )
```

```python
import functools

import jax
import jax.numpy as jnp
from jax import lax
from jax.experimental import pallas as pl
from jax.experimental.pallas import tpu as pltpu
from jax.sharding import PartitionSpec as P

MESH = pl.DeviceIdType.MESH
F32, BF16 = jnp.float32, jnp.bfloat16
HIGHEST = lax.Precision.HIGHEST
TILE = 1024
GROUPS = 4
AXES = ("x", "z", "y")
SLOTS = 3
PHASES = ("core", "line", "plane", "ag_plane", "ag_line", "ag_core")
N_SEMS = 5 + GROUPS * len(PHASES)


def halves(v):
    high = v.astype(BF16)
    return high, (v - high.astype(F32)).astype(BF16)


def thirds(v):
    high = v.astype(BF16)
    rest = v - high.astype(F32)
    mid = rest.astype(BF16)
    return high, mid, (rest - mid.astype(F32)).astype(BF16)


def dot(a, b, ca, cb, precision=None):
    return lax.dot_general(a, b, (((ca,), (cb,)), ((), ())), precision=precision, preferred_element_type=F32)


def kernel(sizes, act_hbm, grad_hbm, res_hbm, query_hbm, res, right,
           act, gbuf, query3, gslice, merged, gq, left, avg, avg2, gram_in, gram_out, gram_slots, chol,
           wl3, tt, core_rx, line_rx, line_sum, plane_rx, last_rx, tf, send, recv, load, gload):
    query = right
    ny, nz, nx = sizes["y"], sizes["z"], sizes["x"]
    dp, tp = lax.axis_index("dp"), lax.axis_index("tp")
    me = {"y": dp, "z": tp // (2 * nx), "x": (tp // 2) % nx}
    core = tp % 2
    rank, width = query_hbm.shape
    tokens, rows = act_hbm.shape
    n_tiles = width // TILE
    gcols = width // GROUPS
    half = rank // 2

    def device(**to):
        at = {**me, "c": core, **to}
        return (at["y"], (at["z"] * nx + at["x"]) * 2 + at["c"])

    def shift(axis, k):
        return lax.rem(me[axis] + k, sizes[axis])

    partner = device(c=1 - core)
    chip = me["z"] * nx + me["x"]
    n_plane = nz * nx
    n_chips = ny * n_plane
    place = dp * n_plane + chip

    def to_plane(b1, b2, act_on):
        n2 = sizes[b2]

        @pl.loop(1, sizes[b1] * n2)
        def _(k):
            p1, p2 = shift(b1, k // n2), shift(b2, k % n2)
            act_on(device(**{b1: p1, b2: p2}), p1 * n2 + p2)

    def to_line(axis, act_on):
        @pl.loop(1, sizes[axis])
        def _(k):
            p = shift(axis, k)
            act_on(device(**{axis: p}), p)

    def to_all(act_on):
        home = ((ny - ny // 2) * nz + nz - nz // 2) * nx + nx - nx // 2

        def step(k):
            y = shift("y", k // n_plane + ny // 2)
            z = shift("z", (k // nx) % nz + nz // 2)
            x = shift("x", k % nx + nx // 2)
            act_on(device(y=y, z=z, x=x), (y * nz + z) * nx + x)

        pl.loop(0, home)(step)
        pl.loop(home + 1, n_chips)(step)

    sent = []

    def remote(src, dst, sem, dev):
        pltpu.make_async_remote_copy(
            src_ref=src, dst_ref=dst, send_sem=send.at[sem], recv_sem=recv.at[sem], device_id=dev, device_id_type=MESH
        ).start()

    def arrived(view, sem):
        pltpu.make_async_copy(view(), view(), recv.at[sem]).wait()
        sent.append((view, sem))

    def at_group(g):
        return pl.ds(gcols * g, gcols)

    def sem_of(g, phase):
        return 5 + g * len(PHASES) + PHASES.index(phase)

    slot = core * n_plane + chip
    slice_rows = tokens // (2 * n_plane)
    loads = [
        pltpu.make_async_copy(query_hbm, query, load.at[0]),
        pltpu.make_async_copy(grad_hbm.at[pl.ds(pl.multiple_of(slot * slice_rows, slice_rows), slice_rows)], gslice, load.at[1]),
        pltpu.make_async_copy(res_hbm, res, load.at[2]),
        pltpu.make_async_copy(act_hbm, act, load.at[3]),
    ]

    def first_load(j):
        cols = pl.ds(pl.multiple_of(j * (TILE // 2), TILE // 2), TILE // 2)
        return pltpu.make_async_copy(grad_hbm.at[:, cols], gbuf.at[0, :, cols], gload.at[SLOTS + j])

    def tile_load(i):
        b = lax.rem(i, SLOTS)
        return pltpu.make_async_copy(grad_hbm.at[:, pl.ds(pl.multiple_of(i * TILE, TILE), TILE)], gbuf.at[b], gload.at[b])

    for c in loads:
        c.start()
    for j in range(2):
        first_load(j).start()
    for b in range(1, SLOTS):
        tile_load(b).start()

    barrier = pltpu.get_barrier_semaphore()

    def greet(dev, _):
        pl.semaphore_signal(barrier, inc=1, device_id=dev, device_id_type=MESH)

    greet(partner, 0)
    to_all(greet)
    n_greet = 1 + n_chips - 1

    loads[0].wait()
    loads[1].wait()

    def fold3(v):
        return v[:rank] + (v[rank:2 * rank] + v[2 * rank:])

    gq_cols = pl.ds(pl.multiple_of(slot * slice_rows, slice_rows), slice_rows)
    gq[:, gq_cols] = jnp.zeros((rank, slice_rows), F32)

    @pl.loop(0, n_tiles)
    def _(i):
        cols = pl.ds(pl.multiple_of(i * TILE, TILE), TILE)
        parts = jnp.concatenate(thirds(query[:, cols]), axis=0)
        query3[:, cols] = parts
        gq[:, gq_cols] += fold3(dot(parts, gslice[:, cols], 1, 1))

    pl.semaphore_wait(barrier, n_greet)
    to_plane("z", "x", lambda dev, _: remote(gq.at[:, gq_cols], gq.at[:, gq_cols], 0, dev))

    loads[2].wait()
    loads[3].wait()

    @pl.loop(0, 2)
    def _(j):
        cols = pl.ds(pl.multiple_of(j * (TILE // 2), TILE // 2), TILE // 2)
        first_load(j).wait()
        merged[:, cols] = dot(act[...], gbuf[0, :, cols], 0, 0) + res[:, cols].astype(F32)

    tile_load(SLOTS).start()

    def tile(i):
        cols = pl.ds(pl.multiple_of(i * TILE, TILE), TILE)
        tile_load(i).wait()
        product = dot(act[...], gbuf[lax.rem(i, SLOTS)], 0, 0)
        merged[:, cols] = product + res[:, cols].astype(F32)

        @pl.when(i + SLOTS < n_tiles)
        def _():
            tile_load(i + SLOTS).start()

    def gq_core():
        arrived(lambda: gq.at[:, pl.ds(0, (n_plane - 1) * slice_rows)], 0)
        mine = gq.at[:, pl.ds(pl.multiple_of(core * n_plane * slice_rows, slice_rows), n_plane * slice_rows)]
        remote(mine, mine, 1, partner)

    def left_factor():
        left[dp] = jnp.zeros((rank, rows), F32)

        @pl.loop(0, n_tiles)
        def _(i):
            cols = pl.ds(pl.multiple_of(i * TILE, TILE), TILE)
            left[dp] += fold3(dot(query3[:, cols], res[:, cols], 1, 1))

        arrived(lambda: gq.at[:, pl.ds(0, n_plane * slice_rows)], 1)
        step = tokens // 4

        @pl.loop(0, 4)
        def _(i):
            part = pl.ds(pl.multiple_of(i * step, step), step)
            left[dp] += fold3(dot(jnp.concatenate(thirds(gq[:, part]), axis=0), act[part, :], 1, 0))

        to_line("y", lambda dev, _: remote(left.at[dp], left.at[dp], 2, dev))

    def average():
        arrived(lambda: left.at[pl.ds(0, ny - 1)], 2)
        total = left[0]
        for r in range(1, ny):
            total = total + left[r]
        total = total * (1.0 / ny)
        avg[...] = total
        high, low = halves(total)
        avg2[:rank] = high
        avg2[rank:] = low
        gram = dot(total, total, 1, 1, HIGHEST)
        gram_out[...] = jnp.concatenate([gram[:half], gram[half:]], axis=1)
        remote(gram_out, gram_in, 3, partner)

    def gram_sum():
        arrived(lambda: gram_in, 3)
        gram_slots[chip] = gram_out[...] + gram_in[...]
        to_plane("z", "x", lambda dev, _: remote(gram_slots.at[chip], gram_slots.at[chip], 4, dev))

    def right_terms(groups):
        step = 2048

        @pl.loop(groups[0] * gcols // step, (groups[-1] + 1) * gcols // step)
        def _(i):
            cols = pl.ds(pl.multiple_of(i * step, step), step)
            high, low = halves(merged[:, cols])
            both = dot(avg2[...], high, 1, 0)
            tt[:, cols] = both[:rank] + (both[rank:] + dot(avg2[:rank], low, 1, 0))

        theirs = pl.ds(pl.multiple_of(half * (1 - core), half), half)
        for g in groups:
            remote(tt.at[theirs, at_group(g)], core_rx.at[:, at_group(g)], sem_of(g, "core"), partner)

    def line_of(g):
        axis = AXES[g]
        b1, b2 = [a for a in ("y", "z", "x") if a != axis]
        n = sizes[axis]
        n_p = sizes[b1] * sizes[b2]
        return axis, b1, b2, n, half // n, me[b1] * sizes[b2] + me[b2], n_p, gcols // n_p

    def part_rows(p, size):
        return pl.ds(pl.multiple_of(p * size, size), size)

    def core_sum(g):
        cols = at_group(g)
        arrived(lambda: core_rx.at[:, cols], sem_of(g, "core"))
        core_rx[:, cols] = core_rx[:, cols] + tt[part_rows(core, half), cols]
        return cols

    n_col = gcols // 128
    l_group = GROUPS - 1
    l_rows = half * gcols // (128 * n_chips)

    def last_piece(at, top):
        return (pl.ds(pl.multiple_of(top + at // n_col * l_rows, l_rows), l_rows),
                pl.ds(pl.multiple_of(gcols * l_group + at % n_col * 128, 128), 128))

    def last_send():
        core_sum(l_group)
        to_all(lambda dev, p: remote(
            core_rx.at[last_piece(p, 0)], last_rx.at[:, part_rows(place, 128)], sem_of(l_group, "line"), dev))

    def last_gather():
        arrived(lambda: last_rx.at[:, pl.ds(0, (n_chips - 1) * 128)], sem_of(l_group, "line"))
        last_rx[:, part_rows(place, 128)] = core_rx[last_piece(place, 0)]
        total = last_rx[:, 0:128]
        for k in range(1, n_chips):
            total = total + last_rx[:, k * 128:(k + 1) * 128]
        piece = last_piece(place, half * core)
        tf[piece] = total
        to_all(lambda dev, _: remote(tf.at[piece], tf.at[piece], sem_of(l_group, "ag_line"), dev))

    def last_core():
        arrived(lambda: tf.at[pl.ds(0, l_rows), pl.ds(0, (n_chips - 1) * 128)], sem_of(l_group, "ag_line"))
        mine = tf.at[part_rows(core, half), at_group(l_group)]
        remote(mine, mine, sem_of(l_group, "ag_core"), partner)

    def line_send(g):
        axis, _, _, n, lrows, *_ = line_of(g)
        cols = core_sum(g)
        to_line(axis, lambda dev, p: remote(
            core_rx.at[part_rows(p, lrows), cols], line_rx.at[g, part_rows(me[axis], lrows)], sem_of(g, "line"), dev))

    def plane_send(g):
        axis, b1, b2, n, lrows, pos, n_p, pcols = line_of(g)
        arrived(lambda: line_rx.at[g, pl.ds(0, (n - 1) * lrows)], sem_of(g, "line"))
        total = core_rx[part_rows(me[axis], lrows), at_group(g)]
        for k in range(1, n):
            total = total + line_rx[g, part_rows(shift(axis, k), lrows)]
        line_sum[g, :lrows] = total
        to_plane(b1, b2, lambda dev, p: remote(
            line_sum.at[g, pl.ds(0, lrows), part_rows(p, pcols)],
            plane_rx.at[g, pl.ds(0, lrows), part_rows(pos, pcols)], sem_of(g, "plane"), dev))

    def gather_plane(g):
        axis, b1, b2, n, lrows, pos, n_p, pcols = line_of(g)
        rest = pl.ds(0, (n_p - 1) * pcols)
        arrived(lambda: plane_rx.at[g, pl.ds(0, lrows), rest], sem_of(g, "plane"))
        mine = part_rows(pos, pcols)
        plane_rx[g, :lrows, mine] = line_sum[g, :lrows, mine]
        total = plane_rx[g, :lrows, 0:pcols]
        for k in range(1, n_p):
            total = total + plane_rx[g, :lrows, k * pcols:(k + 1) * pcols]
        piece = (pl.ds(pl.multiple_of(half * core + lrows * me[axis], lrows), lrows),
                 pl.ds(pl.multiple_of(gcols * g + pcols * pos, pcols), pcols))
        tf[piece] = total
        to_plane(b1, b2, lambda dev, _: remote(tf.at[piece], tf.at[piece], sem_of(g, "ag_plane"), dev))

    def gather_line(g):
        axis, b1, b2, n, lrows, pos, n_p, pcols = line_of(g)
        arrived(lambda: tf.at[pl.ds(0, lrows), pl.ds(0, (n_p - 1) * pcols)], sem_of(g, "ag_plane"))
        piece = (pl.ds(pl.multiple_of(half * core + lrows * me[axis], lrows), lrows), at_group(g))
        to_line(axis, lambda dev, _: remote(tf.at[piece], tf.at[piece], sem_of(g, "ag_line"), dev))

    def gather_core(g):
        axis, b1, b2, n, lrows, *_ = line_of(g)
        arrived(lambda: tf.at[pl.ds(0, (n - 1) * lrows), at_group(g)], sem_of(g, "ag_line"))
        mine = tf.at[part_rows(core, half), at_group(g)]
        remote(mine, mine, sem_of(g, "ag_core"), partner)

    at_row = lax.broadcasted_iota(jnp.int32, (rank, 1), 0)
    at_lane = lax.broadcasted_iota(jnp.int32, (1, 2 * rank), 1)

    def factor_start():
        arrived(lambda: gram_slots.at[pl.ds(0, n_plane - 1)], 4)
        packed = gram_slots[0]
        for k in range(1, n_plane):
            packed = packed + gram_slots[k]
        gram = jnp.concatenate([packed[:, :rank], packed[:, rank:]], axis=0)
        unit = (lax.broadcasted_iota(jnp.int32, (rank, rank), 0) == lax.broadcasted_iota(jnp.int32, (rank, rank), 1)).astype(F32)
        chol[...] = jnp.concatenate([gram, unit], axis=1)

    def factor(start, stop):
        @pl.loop(start, stop)
        def _(k):
            matrix = chol[...]
            row = chol[pl.ds(k, 1), :]
            column = jnp.sum(jnp.where(at_lane == k, matrix, 0.0), axis=1, keepdims=True)
            pivot = jnp.sum(jnp.where(at_lane == k, row, 0.0), axis=1, keepdims=True)
            chol[...] = matrix - jnp.where(at_row > k, column, 0.0) * (row * (1.0 / pivot))

    def factor_end():
        pivots = jnp.sum(jnp.where(at_row == at_lane, chol[...], 0.0), axis=1, keepdims=True)
        inverse = chol[:, rank:] * (1.0 / jnp.sqrt(pivots))
        orth = dot(inverse, avg[...], 1, 0, HIGHEST)
        both = jnp.concatenate([dot(inverse, orth, 0, 0, HIGHEST), inverse.T, jnp.zeros((rank, rank), F32)], axis=1)
        high, low = halves(both * (1.0 / ny))
        wl3[:rank] = high
        wl3[rank:2 * rank] = high
        wl3[2 * rank:] = low

    def finish(g):
        step = 1024
        arrived(lambda: tf.at[pl.ds(0, half), at_group(g)], sem_of(g, "ag_core"))

        @pl.loop(g * gcols // step, (g + 1) * gcols // step)
        def _(i):
            cols = pl.ds(pl.multiple_of(i * step, step), step)
            high, low = halves(tf[:, cols])
            both = dot(wl3[...], jnp.concatenate([high, low, high], axis=0), 0, 0)
            res[:, cols] = (merged[:, cols] - both[:rows]).astype(BF16)
            right[:, cols] = both[rows:rows + rank]

    early = list(range(l_group))

    def after_5():
        average()
        for g in early:
            right_terms([g])
        gram_sum()
        for g in early:
            line_send(g)

    def after_2():
        gq_core()
        left_factor()

    stages = {2: after_2, 5: after_5}

    @pl.loop(1, n_tiles)
    def _(i):
        tile(i)
        for at, stage in stages.items():
            pl.when(i == at)(stage)

    right_terms([l_group])
    plane_send(0)
    plane_send(1)
    plane_send(2)
    last_send()
    factor_start()
    factor(0, rank // 4)
    gather_plane(0)
    gather_plane(1)
    gather_plane(2)
    last_gather()
    factor(rank // 4, rank // 2)
    gather_line(0)
    gather_line(1)
    gather_line(2)
    factor(rank // 2, rank)
    factor_end()
    gather_core(0)
    gather_core(1)
    gather_core(2)
    last_core()
    finish(0)
    finish(1)
    finish(2)
    finish(l_group)
    for view, sem in sent:
        pltpu.make_async_copy(view(), view(), send.at[sem]).wait()


def write_kernel(error, right, error_hbm, right_hbm, sem):
    copies = [pltpu.make_async_copy(error, error_hbm, sem.at[0]), pltpu.make_async_copy(right, right_hbm, sem.at[1])]
    for c in copies:
        c.start()
    for c in copies:
        c.wait()


def solution(mesh):
    n_dp, n_tp = mesh.shape["dp"], mesh.shape["tp"]
    nx = 4 if n_tp == 32 else 2
    sizes = {"y": n_dp, "z": n_tp // (2 * nx), "x": nx}

    def on_device(activations, out_grads, residual, query_factor):
        tokens, rows = activations.shape
        width, rank = query_factor.shape
        half = rank // 2
        gcols = width // GROUPS
        n_plane = sizes["z"] * sizes["x"]
        lmax = half // min(sizes.values())
        error, right_t = pl.pallas_call(
            functools.partial(kernel, sizes),
            out_shape=(pltpu.VMEM((rows, width), BF16), pltpu.VMEM((rank, width), F32)),
            in_specs=[pl.BlockSpec(memory_space=pl.ANY)] * 4,
            out_specs=(pl.BlockSpec(memory_space=pltpu.VMEM),) * 2,
            scratch_shapes=[
                pltpu.VMEM((tokens, rows), BF16),
                pltpu.VMEM((SLOTS, tokens, TILE), BF16),
                pltpu.VMEM((3 * rank, width), BF16),
                pltpu.VMEM((tokens // (2 * n_plane), width), BF16),
                pltpu.VMEM((rows, width), F32),
                pltpu.VMEM((rank, tokens), F32),
                pltpu.VMEM((n_dp, rank, rows), F32),
                pltpu.VMEM((rank, rows), F32),
                pltpu.VMEM((2 * rank, rows), BF16),
                pltpu.VMEM((half, 2 * rank), F32),
                pltpu.VMEM((half, 2 * rank), F32),
                pltpu.VMEM((n_plane, half, 2 * rank), F32),
                pltpu.VMEM((rank, 2 * rank), F32),
                pltpu.VMEM((3 * rank, rows + 2 * rank), BF16),
                pltpu.VMEM((rank, width), F32),
                pltpu.VMEM((half, width), F32),
                pltpu.VMEM((GROUPS, half, gcols), F32),
                pltpu.VMEM((GROUPS, lmax, gcols), F32),
                pltpu.VMEM((GROUPS, lmax, gcols), F32),
                pltpu.VMEM((half * gcols // (128 * sizes["y"] * n_plane), sizes["y"] * n_plane * 128), F32),
                pltpu.VMEM((rank, width), F32),
                pltpu.SemaphoreType.DMA((N_SEMS,)),
                pltpu.SemaphoreType.DMA((N_SEMS,)),
                pltpu.SemaphoreType.DMA((4,)),
                pltpu.SemaphoreType.DMA((SLOTS + 2,)),
            ],
            compiler_params=pltpu.CompilerParams(
                collective_id=0, has_side_effects=True, vmem_limit_bytes=52 * 2**20
            ),
            name="powersgd",
        )(activations, out_grads, residual, query_factor.T)
        error, right_t = pl.pallas_call(
            write_kernel,
            out_shape=(jax.ShapeDtypeStruct((rows, width), BF16), jax.ShapeDtypeStruct((rank, width), F32)),
            in_specs=[pl.BlockSpec(memory_space=pltpu.VMEM)] * 2,
            out_specs=(pl.BlockSpec(memory_space=pl.ANY),) * 2,
            scratch_shapes=[pltpu.SemaphoreType.DMA((2,))],
            compiler_params=pltpu.CompilerParams(vmem_limit_bytes=16 * 2**20),
            name="write_out",
        )(pltpu.with_memory_space_constraint(error, pltpu.VMEM), pltpu.with_memory_space_constraint(right_t, pltpu.VMEM))
        return error, right_t.T

    return jax.shard_map(
        on_device,
        mesh=mesh,
        in_specs=(P("dp", "tp"), P("dp", None), P(("dp", "tp"), None), P()),
        out_specs=(P(("dp", "tp"), None), P()),
        check_vma=False,
    )
```

```python
import functools

import jax
import jax.numpy as jnp
from jax import lax
from jax.experimental import pallas as pl
from jax.experimental.pallas import tpu as pltpu
from jax.sharding import PartitionSpec as P

MESH = pl.DeviceIdType.MESH
F32, BF16 = jnp.float32, jnp.bfloat16
HIGHEST = lax.Precision.HIGHEST
TILE = 1024
GROUPS = 4
AXES = ("x", "z", "y")
SLOTS = 3
PHASES = ("core", "line", "plane", "ag_plane", "ag_line", "ag_core")
N_SEMS = 5 + GROUPS * len(PHASES)


def halves(v):
    high = v.astype(BF16)
    return high, (v - high.astype(F32)).astype(BF16)


def thirds(v):
    high = v.astype(BF16)
    rest = v - high.astype(F32)
    mid = rest.astype(BF16)
    return high, mid, (rest - mid.astype(F32)).astype(BF16)


def dot(a, b, ca, cb, precision=None):
    return lax.dot_general(a, b, (((ca,), (cb,)), ((), ())), precision=precision, preferred_element_type=F32)


def kernel(sizes, act_hbm, grad_hbm, res_hbm, query_hbm, merged, terms3, wl3,
           act, gbuf, res, query, query3, gslice, gq, left, avg, avg2, gram_in, gram_out, gram_slots, chol,
           tt, core_rx, line_rx, line_sum, plane_rx, last_rx, tf, send, recv, load, gload):
    ny, nz, nx = sizes["y"], sizes["z"], sizes["x"]
    dp, tp = lax.axis_index("dp"), lax.axis_index("tp")
    me = {"y": dp, "z": tp // (2 * nx), "x": (tp // 2) % nx}
    core = tp % 2
    rank, width = query_hbm.shape
    tokens, rows = act_hbm.shape
    n_tiles = width // TILE
    gcols = width // GROUPS
    half = rank // 2
    wide = 2048

    def device(**to):
        at = {**me, "c": core, **to}
        return (at["y"], (at["z"] * nx + at["x"]) * 2 + at["c"])

    def shift(axis, k):
        return lax.rem(me[axis] + k, sizes[axis])

    partner = device(c=1 - core)
    chip = me["z"] * nx + me["x"]
    n_plane = nz * nx
    n_chips = ny * n_plane
    place = dp * n_plane + chip

    def to_plane(b1, b2, act_on):
        n2 = sizes[b2]

        @pl.loop(1, sizes[b1] * n2)
        def _(k):
            p1, p2 = shift(b1, k // n2), shift(b2, k % n2)
            act_on(device(**{b1: p1, b2: p2}), p1 * n2 + p2)

    def to_line(axis, act_on):
        @pl.loop(1, sizes[axis])
        def _(k):
            p = shift(axis, k)
            act_on(device(**{axis: p}), p)

    def to_all(act_on):
        home = ((ny - ny // 2) * nz + nz - nz // 2) * nx + nx - nx // 2

        def step(k):
            y = shift("y", k // n_plane + ny // 2)
            z = shift("z", (k // nx) % nz + nz // 2)
            x = shift("x", k % nx + nx // 2)
            act_on(device(y=y, z=z, x=x), (y * nz + z) * nx + x)

        pl.loop(0, home)(step)
        pl.loop(home + 1, n_chips)(step)

    sent = []

    def remote(src, dst, sem, dev):
        pltpu.make_async_remote_copy(
            src_ref=src, dst_ref=dst, send_sem=send.at[sem], recv_sem=recv.at[sem], device_id=dev, device_id_type=MESH
        ).start()

    def arrived(view, sem):
        pltpu.make_async_copy(view(), view(), recv.at[sem]).wait()
        sent.append((view, sem))

    def at_group(g):
        return pl.ds(gcols * g, gcols)

    def sem_of(g, phase):
        return 5 + g * len(PHASES) + PHASES.index(phase)

    slot = core * n_plane + chip
    slice_rows = tokens // (2 * n_plane)
    loads = [
        pltpu.make_async_copy(query_hbm, query, load.at[0]),
        pltpu.make_async_copy(grad_hbm.at[pl.ds(pl.multiple_of(slot * slice_rows, slice_rows), slice_rows)], gslice, load.at[1]),
        pltpu.make_async_copy(res_hbm, res, load.at[2]),
        pltpu.make_async_copy(act_hbm, act, load.at[3]),
    ]

    def first_load(j):
        cols = pl.ds(pl.multiple_of(j * (TILE // 2), TILE // 2), TILE // 2)
        return pltpu.make_async_copy(grad_hbm.at[:, cols], gbuf.at[0, :, cols], gload.at[SLOTS + j])

    def tile_load(i):
        b = lax.rem(i, SLOTS)
        return pltpu.make_async_copy(grad_hbm.at[:, pl.ds(pl.multiple_of(i * TILE, TILE), TILE)], gbuf.at[b], gload.at[b])

    for c in loads:
        c.start()
    for j in range(2):
        first_load(j).start()
    for b in range(1, SLOTS):
        tile_load(b).start()

    barrier = pltpu.get_barrier_semaphore()

    def greet(dev, _):
        pl.semaphore_signal(barrier, inc=1, device_id=dev, device_id_type=MESH)

    greet(partner, 0)
    to_all(greet)
    n_greet = 1 + n_chips - 1

    loads[0].wait()
    loads[1].wait()

    def fold3(v):
        return v[:rank] + (v[rank:2 * rank] + v[2 * rank:])

    gq_cols = pl.ds(pl.multiple_of(slot * slice_rows, slice_rows), slice_rows)
    gq[:, gq_cols] = jnp.zeros((rank, slice_rows), F32)

    @pl.loop(0, width // wide)
    def _(i):
        cols = pl.ds(pl.multiple_of(i * wide, wide), wide)
        parts = jnp.concatenate(thirds(query[:, cols]), axis=0)
        query3[:, cols] = parts
        gq[:, gq_cols] += fold3(dot(parts, gslice[:, cols], 1, 1))

    pl.semaphore_wait(barrier, n_greet)
    to_plane("z", "x", lambda dev, _: remote(gq.at[:, gq_cols], gq.at[:, gq_cols], 0, dev))

    loads[2].wait()
    loads[3].wait()

    @pl.loop(0, 2)
    def _(j):
        cols = pl.ds(pl.multiple_of(j * (TILE // 2), TILE // 2), TILE // 2)
        first_load(j).wait()
        merged[:, cols] = dot(act[...], gbuf[0, :, cols], 0, 0) + res[:, cols].astype(F32)

    tile_load(SLOTS).start()

    def tile(i):
        cols = pl.ds(pl.multiple_of(i * TILE, TILE), TILE)
        tile_load(i).wait()
        product = dot(act[...], gbuf[lax.rem(i, SLOTS)], 0, 0)
        merged[:, cols] = product + res[:, cols].astype(F32)

        @pl.when(i + SLOTS < n_tiles)
        def _():
            tile_load(i + SLOTS).start()

    def gq_core():
        arrived(lambda: gq.at[:, pl.ds(0, (n_plane - 1) * slice_rows)], 0)
        mine = gq.at[:, pl.ds(pl.multiple_of(core * n_plane * slice_rows, slice_rows), n_plane * slice_rows)]
        remote(mine, mine, 1, partner)

    def left_factor():
        left[dp] = jnp.zeros((rank, rows), F32)

        @pl.loop(0, width // wide)
        def _(i):
            cols = pl.ds(pl.multiple_of(i * wide, wide), wide)
            left[dp] += fold3(dot(query3[:, cols], res[:, cols], 1, 1))

        arrived(lambda: gq.at[:, pl.ds(0, n_plane * slice_rows)], 1)
        step = tokens // 2

        @pl.loop(0, 2)
        def _(i):
            part = pl.ds(pl.multiple_of(i * step, step), step)
            left[dp] += fold3(dot(jnp.concatenate(thirds(gq[:, part]), axis=0), act[part, :], 1, 0))

        to_line("y", lambda dev, _: remote(left.at[dp], left.at[dp], 2, dev))

    def average():
        arrived(lambda: left.at[pl.ds(0, ny - 1)], 2)
        total = left[0]
        for r in range(1, ny):
            total = total + left[r]
        total = total * (1.0 / ny)
        avg[...] = total
        high, low = halves(total)
        avg2[:rank] = high
        avg2[rank:] = low
        gram = dot(total, total, 1, 1, HIGHEST)
        gram_out[...] = jnp.concatenate([gram[:half], gram[half:]], axis=1)
        remote(gram_out, gram_in, 3, partner)

    def gram_sum():
        arrived(lambda: gram_in, 3)
        gram_slots[chip] = gram_out[...] + gram_in[...]
        to_plane("z", "x", lambda dev, _: remote(gram_slots.at[chip], gram_slots.at[chip], 4, dev))

    def right_terms(groups):
        step = 2048

        @pl.loop(groups[0] * gcols // step, (groups[-1] + 1) * gcols // step)
        def _(i):
            cols = pl.ds(pl.multiple_of(i * step, step), step)
            high, low = halves(merged[:, cols])
            both = dot(avg2[...], high, 1, 0)
            tt[:, cols] = both[:rank] + (both[rank:] + dot(avg2[:rank], low, 1, 0))

        theirs = pl.ds(pl.multiple_of(half * (1 - core), half), half)
        for g in groups:
            remote(tt.at[theirs, at_group(g)], core_rx.at[:, at_group(g)], sem_of(g, "core"), partner)

    def line_of(g):
        axis = AXES[g]
        b1, b2 = [a for a in ("y", "z", "x") if a != axis]
        n = sizes[axis]
        n_p = sizes[b1] * sizes[b2]
        return axis, b1, b2, n, half // n, me[b1] * sizes[b2] + me[b2], n_p, gcols // n_p

    def part_rows(p, size):
        return pl.ds(pl.multiple_of(p * size, size), size)

    def core_sum(g):
        cols = at_group(g)
        arrived(lambda: core_rx.at[:, cols], sem_of(g, "core"))
        core_rx[:, cols] = core_rx[:, cols] + tt[part_rows(core, half), cols]
        return cols

    n_col = gcols // 128
    l_group = GROUPS - 1
    l_rows = half * gcols // (128 * n_chips)

    def last_piece(at, top):
        return (pl.ds(pl.multiple_of(top + at // n_col * l_rows, l_rows), l_rows),
                pl.ds(pl.multiple_of(gcols * l_group + at % n_col * 128, 128), 128))

    def last_send():
        core_sum(l_group)
        to_all(lambda dev, p: remote(
            core_rx.at[last_piece(p, 0)], last_rx.at[:, part_rows(place, 128)], sem_of(l_group, "line"), dev))

    def last_gather():
        arrived(lambda: last_rx.at[:, pl.ds(0, (n_chips - 1) * 128)], sem_of(l_group, "line"))
        last_rx[:, part_rows(place, 128)] = core_rx[last_piece(place, 0)]
        total = last_rx[:, 0:128]
        for k in range(1, n_chips):
            total = total + last_rx[:, k * 128:(k + 1) * 128]
        piece = last_piece(place, half * core)
        tf[piece] = total
        to_all(lambda dev, _: remote(tf.at[piece], tf.at[piece], sem_of(l_group, "ag_line"), dev))

    def last_core():
        arrived(lambda: tf.at[pl.ds(0, l_rows), pl.ds(0, (n_chips - 1) * 128)], sem_of(l_group, "ag_line"))
        mine = tf.at[part_rows(core, half), at_group(l_group)]
        remote(mine, mine, sem_of(l_group, "ag_core"), partner)

    def line_send(g):
        axis, _, _, n, lrows, *_ = line_of(g)
        cols = core_sum(g)
        to_line(axis, lambda dev, p: remote(
            core_rx.at[part_rows(p, lrows), cols], line_rx.at[g, part_rows(me[axis], lrows)], sem_of(g, "line"), dev))

    def plane_send(g):
        axis, b1, b2, n, lrows, pos, n_p, pcols = line_of(g)
        arrived(lambda: line_rx.at[g, pl.ds(0, (n - 1) * lrows)], sem_of(g, "line"))
        total = core_rx[part_rows(me[axis], lrows), at_group(g)]
        for k in range(1, n):
            total = total + line_rx[g, part_rows(shift(axis, k), lrows)]
        line_sum[g, :lrows] = total
        to_plane(b1, b2, lambda dev, p: remote(
            line_sum.at[g, pl.ds(0, lrows), part_rows(p, pcols)],
            plane_rx.at[g, pl.ds(0, lrows), part_rows(pos, pcols)], sem_of(g, "plane"), dev))

    def gather_plane(g):
        axis, b1, b2, n, lrows, pos, n_p, pcols = line_of(g)
        rest = pl.ds(0, (n_p - 1) * pcols)
        arrived(lambda: plane_rx.at[g, pl.ds(0, lrows), rest], sem_of(g, "plane"))
        mine = part_rows(pos, pcols)
        plane_rx[g, :lrows, mine] = line_sum[g, :lrows, mine]
        total = plane_rx[g, :lrows, 0:pcols]
        for k in range(1, n_p):
            total = total + plane_rx[g, :lrows, k * pcols:(k + 1) * pcols]
        piece = (pl.ds(pl.multiple_of(half * core + lrows * me[axis], lrows), lrows),
                 pl.ds(pl.multiple_of(gcols * g + pcols * pos, pcols), pcols))
        tf[piece] = total
        to_plane(b1, b2, lambda dev, _: remote(tf.at[piece], tf.at[piece], sem_of(g, "ag_plane"), dev))

    def gather_line(g):
        axis, b1, b2, n, lrows, pos, n_p, pcols = line_of(g)
        arrived(lambda: tf.at[pl.ds(0, lrows), pl.ds(0, (n_p - 1) * pcols)], sem_of(g, "ag_plane"))
        piece = (pl.ds(pl.multiple_of(half * core + lrows * me[axis], lrows), lrows), at_group(g))
        to_line(axis, lambda dev, _: remote(tf.at[piece], tf.at[piece], sem_of(g, "ag_line"), dev))

    def gather_core(g):
        axis, b1, b2, n, lrows, *_ = line_of(g)
        arrived(lambda: tf.at[pl.ds(0, (n - 1) * lrows), at_group(g)], sem_of(g, "ag_line"))
        mine = tf.at[part_rows(core, half), at_group(g)]
        remote(mine, mine, sem_of(g, "ag_core"), partner)

    at_row = lax.broadcasted_iota(jnp.int32, (rank, 1), 0)
    at_lane = lax.broadcasted_iota(jnp.int32, (1, 2 * rank), 1)

    def factor_start():
        arrived(lambda: gram_slots.at[pl.ds(0, n_plane - 1)], 4)
        packed = gram_slots[0]
        for k in range(1, n_plane):
            packed = packed + gram_slots[k]
        gram = jnp.concatenate([packed[:, :rank], packed[:, rank:]], axis=0)
        unit = (lax.broadcasted_iota(jnp.int32, (rank, rank), 0) == lax.broadcasted_iota(jnp.int32, (rank, rank), 1)).astype(F32)
        chol[...] = jnp.concatenate([gram, unit], axis=1)

    def factor(start, stop):
        @pl.loop(start, stop)
        def _(k):
            matrix = chol[...]
            row = chol[pl.ds(k, 1), :]
            column = jnp.sum(jnp.where(at_lane == k, matrix, 0.0), axis=1, keepdims=True)
            pivot = jnp.sum(jnp.where(at_lane == k, row, 0.0), axis=1, keepdims=True)
            chol[...] = matrix - jnp.where(at_row > k, column, 0.0) * (row * (1.0 / pivot))

    def factor_end():
        pivots = jnp.sum(jnp.where(at_row == at_lane, chol[...], 0.0), axis=1, keepdims=True)
        inverse = chol[:, rank:] * (1.0 / jnp.sqrt(pivots))
        orth = dot(inverse, avg[...], 1, 0, HIGHEST)
        both = jnp.concatenate([dot(inverse, orth, 0, 0, HIGHEST), inverse.T, jnp.zeros((rank, rank), F32)], axis=1)
        high, low = halves(both * (1.0 / ny))
        wl3[:rank] = high
        wl3[rank:2 * rank] = high
        wl3[2 * rank:] = low

    def finish(g):
        arrived(lambda: tf.at[pl.ds(0, half), at_group(g)], sem_of(g, "ag_core"))
        high, low = halves(tf[:, at_group(g)])
        terms3[:rank, at_group(g)] = high
        terms3[rank:2 * rank, at_group(g)] = low
        terms3[2 * rank:, at_group(g)] = high

    early = list(range(l_group))

    def after_5():
        average()
        for g in early:
            right_terms([g])
        gram_sum()
        for g in early:
            line_send(g)

    def after_2():
        gq_core()
        left_factor()

    stages = {2: after_2, 5: after_5}

    @pl.loop(1, n_tiles)
    def _(i):
        tile(i)
        for at, stage in stages.items():
            pl.when(i == at)(stage)

    right_terms([l_group])
    plane_send(0)
    plane_send(1)
    plane_send(2)
    last_send()
    factor_start()
    factor(0, rank // 4)
    gather_plane(0)
    gather_plane(1)
    gather_plane(2)
    last_gather()
    factor(rank // 4, rank // 2)
    gather_line(0)
    gather_line(1)
    gather_line(2)
    factor(rank // 2, rank)
    factor_end()
    gather_core(0)
    gather_core(1)
    gather_core(2)
    last_core()
    finish(0)
    finish(1)
    finish(2)
    finish(l_group)
    for view, sem in sent:
        pltpu.make_async_copy(view(), view(), send.at[sem]).wait()


def write_kernel(merged, terms3, wl3, error_hbm, right_hbm, error, right, sem):
    rows, width = merged.shape
    rank = right.shape[0]

    def copies(i):
        cols = pl.ds(i * TILE, TILE)
        return (pltpu.make_async_copy(error.at[:, cols], error_hbm.at[:, cols], sem.at[0, i]),
                pltpu.make_async_copy(right.at[:, cols], right_hbm.at[:, cols], sem.at[1, i]))

    for i in range(width // TILE):
        cols = pl.ds(i * TILE, TILE)
        both = dot(wl3[:, :rows + rank], terms3[:, cols], 0, 0)
        error[:, cols] = (merged[:, cols] - both[:rows]).astype(BF16)
        right[:, cols] = both[rows:rows + rank]
        for c in copies(i):
            c.start()

    for i in range(width // TILE):
        for c in copies(i):
            c.wait()


def solution(mesh):
    n_dp, n_tp = mesh.shape["dp"], mesh.shape["tp"]
    nx = 4 if n_tp == 32 else 2
    sizes = {"y": n_dp, "z": n_tp // (2 * nx), "x": nx}

    def on_device(activations, out_grads, residual, query_factor):
        tokens, rows = activations.shape
        width, rank = query_factor.shape
        half = rank // 2
        gcols = width // GROUPS
        n_plane = sizes["z"] * sizes["x"]
        lmax = half // min(sizes.values())
        merged, terms3, wl3 = pl.pallas_call(
            functools.partial(kernel, sizes),
            out_shape=(
                pltpu.VMEM((rows, width), F32),
                pltpu.VMEM((3 * rank, width), BF16),
                pltpu.VMEM((3 * rank, rows + 2 * rank), BF16),
            ),
            in_specs=[pl.BlockSpec(memory_space=pl.ANY)] * 4,
            out_specs=(pl.BlockSpec(memory_space=pltpu.VMEM),) * 3,
            scratch_shapes=[
                pltpu.VMEM((tokens, rows), BF16),
                pltpu.VMEM((SLOTS, tokens, TILE), BF16),
                pltpu.VMEM((rows, width), BF16),
                pltpu.VMEM((rank, width), F32),
                pltpu.VMEM((3 * rank, width), BF16),
                pltpu.VMEM((tokens // (2 * n_plane), width), BF16),
                pltpu.VMEM((rank, tokens), F32),
                pltpu.VMEM((n_dp, rank, rows), F32),
                pltpu.VMEM((rank, rows), F32),
                pltpu.VMEM((2 * rank, rows), BF16),
                pltpu.VMEM((half, 2 * rank), F32),
                pltpu.VMEM((half, 2 * rank), F32),
                pltpu.VMEM((n_plane, half, 2 * rank), F32),
                pltpu.VMEM((rank, 2 * rank), F32),
                pltpu.VMEM((rank, width), F32),
                pltpu.VMEM((half, width), F32),
                pltpu.VMEM((GROUPS, half, gcols), F32),
                pltpu.VMEM((GROUPS, lmax, gcols), F32),
                pltpu.VMEM((GROUPS, lmax, gcols), F32),
                pltpu.VMEM((half * gcols // (128 * sizes["y"] * n_plane), sizes["y"] * n_plane * 128), F32),
                pltpu.VMEM((rank, width), F32),
                pltpu.SemaphoreType.DMA((N_SEMS,)),
                pltpu.SemaphoreType.DMA((N_SEMS,)),
                pltpu.SemaphoreType.DMA((4,)),
                pltpu.SemaphoreType.DMA((SLOTS + 2,)),
            ],
            compiler_params=pltpu.CompilerParams(
                collective_id=0, has_side_effects=True, vmem_limit_bytes=50 * 2**20
            ),
            name="powersgd",
        )(activations, out_grads, residual, query_factor.T)
        error, right_t = pl.pallas_call(
            write_kernel,
            out_shape=(jax.ShapeDtypeStruct((rows, width), BF16), jax.ShapeDtypeStruct((rank, width), F32)),
            in_specs=[pl.BlockSpec(memory_space=pltpu.VMEM)] * 3,
            out_specs=(pl.BlockSpec(memory_space=pl.ANY),) * 2,
            scratch_shapes=[
                pltpu.VMEM((rows, width), BF16),
                pltpu.VMEM((rank, width), F32),
                pltpu.SemaphoreType.DMA((2, width // TILE)),
            ],
            compiler_params=pltpu.CompilerParams(vmem_limit_bytes=24 * 2**20),
            name="finish",
        )(*(pltpu.with_memory_space_constraint(v, pltpu.VMEM) for v in (merged, terms3, wl3)))
        return error, right_t.T

    return jax.shard_map(
        on_device,
        mesh=mesh,
        in_specs=(P("dp", "tp"), P("dp", None), P(("dp", "tp"), None), P()),
        out_specs=(P(("dp", "tp"), None), P()),
        check_vma=False,
    )
```

```python
import functools

import jax
import jax.numpy as jnp
from jax import lax
from jax.experimental import pallas as pl
from jax.experimental.pallas import tpu as pltpu
from jax.sharding import PartitionSpec as P

MESH = pl.DeviceIdType.MESH
F32, BF16 = jnp.float32, jnp.bfloat16
HIGHEST = lax.Precision.HIGHEST
TILE = 1024
GROUPS = 4
AXES = ("x", "z", "y")
SLOTS = 3
PHASES = ("core", "line", "plane", "ag_plane", "ag_line", "ag_core")
N_SEMS = 5 + GROUPS * len(PHASES)


def halves(v):
    high = v.astype(BF16)
    return high, (v - high.astype(F32)).astype(BF16)


def thirds(v):
    high = v.astype(BF16)
    rest = v - high.astype(F32)
    mid = rest.astype(BF16)
    return high, mid, (rest - mid.astype(F32)).astype(BF16)


def dot(a, b, ca, cb, precision=None):
    return lax.dot_general(a, b, (((ca,), (cb,)), ((), ())), precision=precision, preferred_element_type=F32)


def kernel(sizes, act_hbm, grad_hbm, res_hbm, query_hbm, merged, terms3, wl3,
           act, gbuf, res, query, query3, gslice, gq, left, avg, avg2, gram_in, gram_out, gram_slots, chol,
           tt, core_rx, line_rx, line_sum, plane_rx, last_rx, tf, send, recv, load, gload):
    ny, nz, nx = sizes["y"], sizes["z"], sizes["x"]
    dp, tp = lax.axis_index("dp"), lax.axis_index("tp")
    me = {"y": dp, "z": tp // (2 * nx), "x": (tp // 2) % nx}
    core = tp % 2
    rank, width = query_hbm.shape
    tokens, rows = act_hbm.shape
    n_tiles = width // TILE
    gcols = width // GROUPS
    half = rank // 2
    wide = 2048

    def device(**to):
        at = {**me, "c": core, **to}
        return (at["y"], (at["z"] * nx + at["x"]) * 2 + at["c"])

    def shift(axis, k):
        return lax.rem(me[axis] + k, sizes[axis])

    partner = device(c=1 - core)
    chip = me["z"] * nx + me["x"]
    n_plane = nz * nx
    n_chips = ny * n_plane
    place = dp * n_plane + chip

    def to_plane(b1, b2, act_on):
        n1, n2 = sizes[b1], sizes[b2]
        home = (n1 - n1 // 2) * n2 + n2 - n2 // 2

        def step(k):
            p1, p2 = shift(b1, k // n2 + n1 // 2), shift(b2, k % n2 + n2 // 2)
            act_on(device(**{b1: p1, b2: p2}), p1 * n2 + p2)

        pl.loop(0, home)(step)
        pl.loop(home + 1, n1 * n2)(step)

    def to_line(axis, act_on):
        @pl.loop(1, sizes[axis])
        def _(k):
            p = shift(axis, k)
            act_on(device(**{axis: p}), p)

    def to_all(act_on):
        home = ((ny - ny // 2) * nz + nz - nz // 2) * nx + nx - nx // 2

        def step(k):
            y = shift("y", k // n_plane + ny // 2)
            z = shift("z", (k // nx) % nz + nz // 2)
            x = shift("x", k % nx + nx // 2)
            act_on(device(y=y, z=z, x=x), (y * nz + z) * nx + x)

        pl.loop(0, home)(step)
        pl.loop(home + 1, n_chips)(step)

    sent = []

    def remote(src, dst, sem, dev):
        pltpu.make_async_remote_copy(
            src_ref=src, dst_ref=dst, send_sem=send.at[sem], recv_sem=recv.at[sem], device_id=dev, device_id_type=MESH
        ).start()

    def arrived(view, sem):
        pltpu.make_async_copy(view(), view(), recv.at[sem]).wait()
        sent.append((view, sem))

    def at_group(g):
        return pl.ds(gcols * g, gcols)

    def sem_of(g, phase):
        return 5 + g * len(PHASES) + PHASES.index(phase)

    slot = core * n_plane + chip
    slice_rows = tokens // (2 * n_plane)
    loads = [
        pltpu.make_async_copy(query_hbm, query, load.at[0]),
        pltpu.make_async_copy(grad_hbm.at[pl.ds(pl.multiple_of(slot * slice_rows, slice_rows), slice_rows)], gslice, load.at[1]),
        pltpu.make_async_copy(res_hbm, res, load.at[2]),
        pltpu.make_async_copy(act_hbm, act, load.at[3]),
    ]

    def first_load(j):
        cols = pl.ds(pl.multiple_of(j * (TILE // 2), TILE // 2), TILE // 2)
        return pltpu.make_async_copy(grad_hbm.at[:, cols], gbuf.at[0, :, cols], gload.at[SLOTS + j])

    def tile_load(i):
        b = lax.rem(i, SLOTS)
        return pltpu.make_async_copy(grad_hbm.at[:, pl.ds(pl.multiple_of(i * TILE, TILE), TILE)], gbuf.at[b], gload.at[b])

    for c in loads:
        c.start()
    for j in range(2):
        first_load(j).start()
    for b in range(1, SLOTS):
        tile_load(b).start()

    barrier = pltpu.get_barrier_semaphore()

    def greet(dev, _):
        pl.semaphore_signal(barrier, inc=1, device_id=dev, device_id_type=MESH)

    greet(partner, 0)
    to_all(greet)
    n_greet = 1 + n_chips - 1

    loads[0].wait()
    loads[1].wait()

    def fold3(v):
        return v[:rank] + (v[rank:2 * rank] + v[2 * rank:])

    gq_cols = pl.ds(pl.multiple_of(slot * slice_rows, slice_rows), slice_rows)
    gq[:, gq_cols] = jnp.zeros((rank, slice_rows), F32)

    @pl.loop(0, width // wide)
    def _(i):
        cols = pl.ds(pl.multiple_of(i * wide, wide), wide)
        parts = jnp.concatenate(thirds(query[:, cols]), axis=0)
        query3[:, cols] = parts
        gq[:, gq_cols] += fold3(dot(parts, gslice[:, cols], 1, 1))

    pl.semaphore_wait(barrier, n_greet)
    to_plane("z", "x", lambda dev, _: remote(gq.at[:, gq_cols], gq.at[:, gq_cols], 0, dev))

    loads[2].wait()
    loads[3].wait()

    @pl.loop(0, 2)
    def _(j):
        cols = pl.ds(pl.multiple_of(j * (TILE // 2), TILE // 2), TILE // 2)
        first_load(j).wait()
        merged[:, cols] = dot(act[...], gbuf[0, :, cols], 0, 0) + res[:, cols].astype(F32)

    tile_load(SLOTS).start()

    def tile(i):
        cols = pl.ds(pl.multiple_of(i * TILE, TILE), TILE)
        tile_load(i).wait()
        product = dot(act[...], gbuf[lax.rem(i, SLOTS)], 0, 0)
        merged[:, cols] = product + res[:, cols].astype(F32)

        @pl.when(i + SLOTS < n_tiles)
        def _():
            tile_load(i + SLOTS).start()

    def gq_core():
        arrived(lambda: gq.at[:, pl.ds(0, (n_plane - 1) * slice_rows)], 0)
        mine = gq.at[:, pl.ds(pl.multiple_of(core * n_plane * slice_rows, slice_rows), n_plane * slice_rows)]
        remote(mine, mine, 1, partner)

    def left_factor():
        left[dp] = jnp.zeros((rank, rows), F32)

        @pl.loop(0, width // wide)
        def _(i):
            cols = pl.ds(pl.multiple_of(i * wide, wide), wide)
            left[dp] += fold3(dot(query3[:, cols], res[:, cols], 1, 1))

        arrived(lambda: gq.at[:, pl.ds(0, n_plane * slice_rows)], 1)
        step = tokens // 2

        @pl.loop(0, 2)
        def _(i):
            part = pl.ds(pl.multiple_of(i * step, step), step)
            left[dp] += fold3(dot(jnp.concatenate(thirds(gq[:, part]), axis=0), act[part, :], 1, 0))

        to_line("y", lambda dev, _: remote(left.at[dp], left.at[dp], 2, dev))

    def average():
        arrived(lambda: left.at[pl.ds(0, ny - 1)], 2)
        total = left[0]
        for r in range(1, ny):
            total = total + left[r]
        total = total * (1.0 / ny)
        avg[...] = total
        high, low = halves(total)
        avg2[:rank] = high
        avg2[rank:] = low
        gram = dot(total, total, 1, 1, HIGHEST)
        gram_out[...] = jnp.concatenate([gram[:half], gram[half:]], axis=1)
        remote(gram_out, gram_in, 3, partner)

    def gram_sum():
        arrived(lambda: gram_in, 3)
        gram_slots[chip] = gram_out[...] + gram_in[...]
        to_plane("z", "x", lambda dev, _: remote(gram_slots.at[chip], gram_slots.at[chip], 4, dev))

    def right_terms(groups):
        step = 2048

        @pl.loop(groups[0] * gcols // step, (groups[-1] + 1) * gcols // step)
        def _(i):
            cols = pl.ds(pl.multiple_of(i * step, step), step)
            high, low = halves(merged[:, cols])
            both = dot(avg2[...], high, 1, 0)
            tt[:, cols] = both[:rank] + (both[rank:] + dot(avg2[:rank], low, 1, 0))

        theirs = pl.ds(pl.multiple_of(half * (1 - core), half), half)
        for g in groups:
            remote(tt.at[theirs, at_group(g)], core_rx.at[:, at_group(g)], sem_of(g, "core"), partner)

    def line_of(g):
        axis = AXES[g]
        b1, b2 = [a for a in ("y", "z", "x") if a != axis]
        n = sizes[axis]
        n_p = sizes[b1] * sizes[b2]
        return axis, b1, b2, n, half // n, me[b1] * sizes[b2] + me[b2], n_p, gcols // n_p

    def part_rows(p, size):
        return pl.ds(pl.multiple_of(p * size, size), size)

    def core_sum(g):
        cols = at_group(g)
        arrived(lambda: core_rx.at[:, cols], sem_of(g, "core"))
        core_rx[:, cols] = core_rx[:, cols] + tt[part_rows(core, half), cols]
        return cols

    n_col = gcols // 128
    l_group = GROUPS - 1
    l_rows = half * gcols // (128 * n_chips)

    def last_piece(at, top):
        return (pl.ds(pl.multiple_of(top + at // n_col * l_rows, l_rows), l_rows),
                pl.ds(pl.multiple_of(gcols * l_group + at % n_col * 128, 128), 128))

    def last_send():
        core_sum(l_group)
        to_all(lambda dev, p: remote(
            core_rx.at[last_piece(p, 0)], last_rx.at[:, part_rows(place, 128)], sem_of(l_group, "line"), dev))

    def last_gather():
        arrived(lambda: last_rx.at[:, pl.ds(0, (n_chips - 1) * 128)], sem_of(l_group, "line"))
        last_rx[:, part_rows(place, 128)] = core_rx[last_piece(place, 0)]
        total = last_rx[:, 0:128]
        for k in range(1, n_chips):
            total = total + last_rx[:, k * 128:(k + 1) * 128]
        piece = last_piece(place, half * core)
        tf[piece] = total
        to_all(lambda dev, _: remote(tf.at[piece], tf.at[piece], sem_of(l_group, "ag_line"), dev))

    def last_core():
        arrived(lambda: tf.at[pl.ds(0, l_rows), pl.ds(0, (n_chips - 1) * 128)], sem_of(l_group, "ag_line"))
        mine = tf.at[part_rows(core, half), at_group(l_group)]
        remote(mine, mine, sem_of(l_group, "ag_core"), partner)

    def line_send(g):
        axis, _, _, n, lrows, *_ = line_of(g)
        cols = core_sum(g)
        to_line(axis, lambda dev, p: remote(
            core_rx.at[part_rows(p, lrows), cols], line_rx.at[g, part_rows(me[axis], lrows)], sem_of(g, "line"), dev))

    def plane_send(g):
        axis, b1, b2, n, lrows, pos, n_p, pcols = line_of(g)
        arrived(lambda: line_rx.at[g, pl.ds(0, (n - 1) * lrows)], sem_of(g, "line"))
        total = core_rx[part_rows(me[axis], lrows), at_group(g)]
        for k in range(1, n):
            total = total + line_rx[g, part_rows(shift(axis, k), lrows)]
        line_sum[g, :lrows] = total
        to_plane(b1, b2, lambda dev, p: remote(
            line_sum.at[g, pl.ds(0, lrows), part_rows(p, pcols)],
            plane_rx.at[g, pl.ds(0, lrows), part_rows(pos, pcols)], sem_of(g, "plane"), dev))

    def gather_plane(g):
        axis, b1, b2, n, lrows, pos, n_p, pcols = line_of(g)
        rest = pl.ds(0, (n_p - 1) * pcols)
        arrived(lambda: plane_rx.at[g, pl.ds(0, lrows), rest], sem_of(g, "plane"))
        mine = part_rows(pos, pcols)
        plane_rx[g, :lrows, mine] = line_sum[g, :lrows, mine]
        total = plane_rx[g, :lrows, 0:pcols]
        for k in range(1, n_p):
            total = total + plane_rx[g, :lrows, k * pcols:(k + 1) * pcols]
        piece = (pl.ds(pl.multiple_of(half * core + lrows * me[axis], lrows), lrows),
                 pl.ds(pl.multiple_of(gcols * g + pcols * pos, pcols), pcols))
        tf[piece] = total
        to_plane(b1, b2, lambda dev, _: remote(tf.at[piece], tf.at[piece], sem_of(g, "ag_plane"), dev))

    def gather_line(g):
        axis, b1, b2, n, lrows, pos, n_p, pcols = line_of(g)
        arrived(lambda: tf.at[pl.ds(0, lrows), pl.ds(0, (n_p - 1) * pcols)], sem_of(g, "ag_plane"))
        piece = (pl.ds(pl.multiple_of(half * core + lrows * me[axis], lrows), lrows), at_group(g))
        to_line(axis, lambda dev, _: remote(tf.at[piece], tf.at[piece], sem_of(g, "ag_line"), dev))

    def gather_core(g):
        axis, b1, b2, n, lrows, *_ = line_of(g)
        arrived(lambda: tf.at[pl.ds(0, (n - 1) * lrows), at_group(g)], sem_of(g, "ag_line"))
        mine = tf.at[part_rows(core, half), at_group(g)]
        remote(mine, mine, sem_of(g, "ag_core"), partner)

    at_row = lax.broadcasted_iota(jnp.int32, (rank, 1), 0)
    at_lane = lax.broadcasted_iota(jnp.int32, (1, 2 * rank), 1)

    def factor_start():
        arrived(lambda: gram_slots.at[pl.ds(0, n_plane - 1)], 4)
        packed = gram_slots[0]
        for k in range(1, n_plane):
            packed = packed + gram_slots[k]
        gram = jnp.concatenate([packed[:, :rank], packed[:, rank:]], axis=0)
        unit = (lax.broadcasted_iota(jnp.int32, (rank, rank), 0) == lax.broadcasted_iota(jnp.int32, (rank, rank), 1)).astype(F32)
        chol[...] = jnp.concatenate([gram, unit], axis=1)

    def factor(start, stop):
        @pl.loop(start, stop)
        def _(k):
            matrix = chol[...]
            row = chol[pl.ds(k, 1), :]
            column = jnp.sum(jnp.where(at_lane == k, matrix, 0.0), axis=1, keepdims=True)
            pivot = jnp.sum(jnp.where(at_lane == k, row, 0.0), axis=1, keepdims=True)
            chol[...] = matrix - jnp.where(at_row > k, column, 0.0) * (row * (1.0 / pivot))

    def factor_end():
        pivots = jnp.sum(jnp.where(at_row == at_lane, chol[...], 0.0), axis=1, keepdims=True)
        inverse = chol[:, rank:] * (1.0 / jnp.sqrt(pivots))
        orth = dot(inverse, avg[...], 1, 0, HIGHEST)
        both = jnp.concatenate([dot(inverse, orth, 0, 0, HIGHEST), inverse.T, jnp.zeros((rank, rank), F32)], axis=1)
        high, low = halves(both * (1.0 / ny))
        wl3[:rank] = high
        wl3[rank:2 * rank] = high
        wl3[2 * rank:] = low

    def finish(g):
        arrived(lambda: tf.at[pl.ds(0, half), at_group(g)], sem_of(g, "ag_core"))
        high, low = halves(tf[:, at_group(g)])
        terms3[:rank, at_group(g)] = high
        terms3[rank:2 * rank, at_group(g)] = low
        terms3[2 * rank:, at_group(g)] = high

    early = list(range(l_group))

    def after_5():
        average()
        right_terms([0])
        right_terms([1])
        line_send(0)
        right_terms([2])
        line_send(1)
        gram_sum()
        line_send(2)

    def after_2():
        gq_core()
        left_factor()

    stages = {2: after_2, 5: after_5}

    @pl.loop(1, n_tiles)
    def _(i):
        tile(i)
        for at, stage in stages.items():
            pl.when(i == at)(stage)

    right_terms([l_group])
    plane_send(0)
    plane_send(1)
    plane_send(2)
    last_send()
    factor_start()
    factor(0, rank // 4)
    gather_plane(0)
    gather_plane(1)
    gather_plane(2)
    last_gather()
    factor(rank // 4, rank // 2)
    gather_line(0)
    gather_line(1)
    gather_line(2)
    factor(rank // 2, rank)
    factor_end()
    gather_core(0)
    gather_core(1)
    gather_core(2)
    last_core()
    finish(0)
    finish(1)
    finish(2)
    finish(l_group)
    for view, sem in sent:
        pltpu.make_async_copy(view(), view(), send.at[sem]).wait()


def write_kernel(merged, terms3, wl3, error_hbm, right_hbm, error, right, sem):
    rows, width = merged.shape
    rank = right.shape[0]

    def copies(i):
        cols = pl.ds(i * TILE, TILE)
        return (pltpu.make_async_copy(error.at[:, cols], error_hbm.at[:, cols], sem.at[0, i]),
                pltpu.make_async_copy(right.at[:, cols], right_hbm.at[:, cols], sem.at[1, i]))

    for i in range(width // TILE):
        cols = pl.ds(i * TILE, TILE)
        both = dot(wl3[:, :rows + rank], terms3[:, cols], 0, 0)
        error[:, cols] = (merged[:, cols] - both[:rows]).astype(BF16)
        right[:, cols] = both[rows:rows + rank]
        for c in copies(i):
            c.start()

    for i in range(width // TILE):
        for c in copies(i):
            c.wait()


def solution(mesh):
    n_dp, n_tp = mesh.shape["dp"], mesh.shape["tp"]
    nx = 4 if n_tp == 32 else 2
    sizes = {"y": n_dp, "z": n_tp // (2 * nx), "x": nx}

    def on_device(activations, out_grads, residual, query_factor):
        tokens, rows = activations.shape
        width, rank = query_factor.shape
        half = rank // 2
        gcols = width // GROUPS
        n_plane = sizes["z"] * sizes["x"]
        lmax = half // min(sizes.values())
        merged, terms3, wl3 = pl.pallas_call(
            functools.partial(kernel, sizes),
            out_shape=(
                pltpu.VMEM((rows, width), F32),
                pltpu.VMEM((3 * rank, width), BF16),
                pltpu.VMEM((3 * rank, rows + 2 * rank), BF16),
            ),
            in_specs=[pl.BlockSpec(memory_space=pl.ANY)] * 4,
            out_specs=(pl.BlockSpec(memory_space=pltpu.VMEM),) * 3,
            scratch_shapes=[
                pltpu.VMEM((tokens, rows), BF16),
                pltpu.VMEM((SLOTS, tokens, TILE), BF16),
                pltpu.VMEM((rows, width), BF16),
                pltpu.VMEM((rank, width), F32),
                pltpu.VMEM((3 * rank, width), BF16),
                pltpu.VMEM((tokens // (2 * n_plane), width), BF16),
                pltpu.VMEM((rank, tokens), F32),
                pltpu.VMEM((n_dp, rank, rows), F32),
                pltpu.VMEM((rank, rows), F32),
                pltpu.VMEM((2 * rank, rows), BF16),
                pltpu.VMEM((half, 2 * rank), F32),
                pltpu.VMEM((half, 2 * rank), F32),
                pltpu.VMEM((n_plane, half, 2 * rank), F32),
                pltpu.VMEM((rank, 2 * rank), F32),
                pltpu.VMEM((rank, width), F32),
                pltpu.VMEM((half, width), F32),
                pltpu.VMEM((GROUPS, half, gcols), F32),
                pltpu.VMEM((GROUPS, lmax, gcols), F32),
                pltpu.VMEM((GROUPS, lmax, gcols), F32),
                pltpu.VMEM((half * gcols // (128 * sizes["y"] * n_plane), sizes["y"] * n_plane * 128), F32),
                pltpu.VMEM((rank, width), F32),
                pltpu.SemaphoreType.DMA((N_SEMS,)),
                pltpu.SemaphoreType.DMA((N_SEMS,)),
                pltpu.SemaphoreType.DMA((4,)),
                pltpu.SemaphoreType.DMA((SLOTS + 2,)),
            ],
            compiler_params=pltpu.CompilerParams(
                collective_id=0, has_side_effects=True, vmem_limit_bytes=50 * 2**20
            ),
            name="powersgd",
        )(activations, out_grads, residual, query_factor.T)
        error, right_t = pl.pallas_call(
            write_kernel,
            out_shape=(jax.ShapeDtypeStruct((rows, width), BF16), jax.ShapeDtypeStruct((rank, width), F32)),
            in_specs=[pl.BlockSpec(memory_space=pltpu.VMEM)] * 3,
            out_specs=(pl.BlockSpec(memory_space=pl.ANY),) * 2,
            scratch_shapes=[
                pltpu.VMEM((rows, width), BF16),
                pltpu.VMEM((rank, width), F32),
                pltpu.SemaphoreType.DMA((2, width // TILE)),
            ],
            compiler_params=pltpu.CompilerParams(vmem_limit_bytes=24 * 2**20),
            name="finish",
        )(*(pltpu.with_memory_space_constraint(v, pltpu.VMEM) for v in (merged, terms3, wl3)))
        return error, right_t.T

    return jax.shard_map(
        on_device,
        mesh=mesh,
        in_specs=(P("dp", "tp"), P("dp", None), P(("dp", "tp"), None), P()),
        out_specs=(P(("dp", "tp"), None), P()),
        check_vma=False,
    )
```

```python
import functools

import jax
import jax.numpy as jnp
from jax import lax
from jax.experimental import pallas as pl
from jax.experimental.pallas import tpu as pltpu
from jax.sharding import PartitionSpec as P

MESH = pl.DeviceIdType.MESH
F32, BF16 = jnp.float32, jnp.bfloat16
HIGHEST = lax.Precision.HIGHEST
TILE = 1024
GROUPS = 4
AXES = ("x", "z", "y")
SLOTS = 3
PHASES = ("core", "line", "plane", "ag_plane", "ag_line", "ag_core")
N_SEMS = 5 + GROUPS * len(PHASES)


def halves(v):
    high = v.astype(BF16)
    return high, (v - high.astype(F32)).astype(BF16)


def thirds(v):
    high = v.astype(BF16)
    rest = v - high.astype(F32)
    mid = rest.astype(BF16)
    return high, mid, (rest - mid.astype(F32)).astype(BF16)


def dot(a, b, ca, cb, precision=None):
    return lax.dot_general(a, b, (((ca,), (cb,)), ((), ())), precision=precision, preferred_element_type=F32)


def kernel(sizes, act_hbm, grad_hbm, res_hbm, query_hbm, merged, terms3, wl3,
           act, gbuf, res, query, query3, gslice, gq, left, avg, avg2, gram_in, gram_out, gram_slots, chol,
           tt, core_rx, line_rx, line_sum, plane_rx, last_rx, tf, send, recv, load, gload):
    ny, nz, nx = sizes["y"], sizes["z"], sizes["x"]
    dp, tp = lax.axis_index("dp"), lax.axis_index("tp")
    me = {"y": dp, "z": tp // (2 * nx), "x": (tp // 2) % nx}
    core = tp % 2
    rank, width = query_hbm.shape
    tokens, rows = act_hbm.shape
    n_tiles = width // TILE
    gcols = width // GROUPS
    half = rank // 2
    wide = 2048

    def device(**to):
        at = {**me, "c": core, **to}
        return (at["y"], (at["z"] * nx + at["x"]) * 2 + at["c"])

    def shift(axis, k):
        return lax.rem(me[axis] + k, sizes[axis])

    partner = device(c=1 - core)
    chip = me["z"] * nx + me["x"]
    n_plane = nz * nx
    n_chips = ny * n_plane
    place = dp * n_plane + chip

    def to_plane(b1, b2, act_on):
        n1, n2 = sizes[b1], sizes[b2]
        home = (n1 - n1 // 2) * n2 + n2 - n2 // 2

        def step(k):
            p1, p2 = shift(b1, k // n2 + n1 // 2), shift(b2, k % n2 + n2 // 2)
            act_on(device(**{b1: p1, b2: p2}), p1 * n2 + p2)

        pl.loop(0, home)(step)
        pl.loop(home + 1, n1 * n2)(step)

    def to_line(axis, act_on):
        @pl.loop(1, sizes[axis])
        def _(k):
            p = shift(axis, k)
            act_on(device(**{axis: p}), p)

    def to_all(act_on):
        home = ((ny - ny // 2) * nz + nz - nz // 2) * nx + nx - nx // 2

        def step(k):
            y = shift("y", k // n_plane + ny // 2)
            z = shift("z", (k // nx) % nz + nz // 2)
            x = shift("x", k % nx + nx // 2)
            act_on(device(y=y, z=z, x=x), (y * nz + z) * nx + x)

        pl.loop(0, home)(step)
        pl.loop(home + 1, n_chips)(step)

    sent = []

    def remote(src, dst, sem, dev):
        pltpu.make_async_remote_copy(
            src_ref=src, dst_ref=dst, send_sem=send.at[sem], recv_sem=recv.at[sem], device_id=dev, device_id_type=MESH
        ).start()

    def arrived(view, sem):
        pltpu.make_async_copy(view(), view(), recv.at[sem]).wait()
        sent.append((view, sem))

    def at_group(g):
        return pl.ds(gcols * g, gcols)

    def sem_of(g, phase):
        return 5 + g * len(PHASES) + PHASES.index(phase)

    slot = core * n_plane + chip
    slice_rows = tokens // (2 * n_plane)
    loads = [
        pltpu.make_async_copy(query_hbm, query, load.at[0]),
        pltpu.make_async_copy(grad_hbm.at[pl.ds(pl.multiple_of(slot * slice_rows, slice_rows), slice_rows)], gslice, load.at[1]),
        pltpu.make_async_copy(res_hbm, res, load.at[2]),
        pltpu.make_async_copy(act_hbm, act, load.at[3]),
    ]

    def first_load(j):
        cols = pl.ds(pl.multiple_of(j * (TILE // 2), TILE // 2), TILE // 2)
        return pltpu.make_async_copy(grad_hbm.at[:, cols], gbuf.at[0, :, cols], gload.at[SLOTS + j])

    def tile_load(i):
        b = lax.rem(i, SLOTS)
        return pltpu.make_async_copy(grad_hbm.at[:, pl.ds(pl.multiple_of(i * TILE, TILE), TILE)], gbuf.at[b], gload.at[b])

    for c in loads:
        c.start()
    for j in range(2):
        first_load(j).start()
    for b in range(1, SLOTS):
        tile_load(b).start()

    barrier = pltpu.get_barrier_semaphore()

    def greet(dev, _):
        pl.semaphore_signal(barrier, inc=1, device_id=dev, device_id_type=MESH)

    greet(partner, 0)
    to_all(greet)
    n_greet = 1 + n_chips - 1

    loads[0].wait()
    loads[1].wait()

    def fold3(v):
        return v[:rank] + (v[rank:2 * rank] + v[2 * rank:])

    gq_cols = pl.ds(pl.multiple_of(slot * slice_rows, slice_rows), slice_rows)
    gq[:, gq_cols] = jnp.zeros((rank, slice_rows), F32)

    @pl.loop(0, width // wide)
    def _(i):
        cols = pl.ds(pl.multiple_of(i * wide, wide), wide)
        parts = jnp.concatenate(thirds(query[:, cols]), axis=0)
        query3[:, cols] = parts
        gq[:, gq_cols] += fold3(dot(parts, gslice[:, cols], 1, 1))

    pl.semaphore_wait(barrier, n_greet)
    to_plane("z", "x", lambda dev, _: remote(gq.at[:, gq_cols], gq.at[:, gq_cols], 0, dev))

    loads[2].wait()
    loads[3].wait()

    @pl.loop(0, 2)
    def _(j):
        cols = pl.ds(pl.multiple_of(j * (TILE // 2), TILE // 2), TILE // 2)
        first_load(j).wait()
        merged[:, cols] = dot(act[...], gbuf[0, :, cols], 0, 0) + res[:, cols].astype(F32)

    tile_load(SLOTS).start()

    def tile(i):
        cols = pl.ds(pl.multiple_of(i * TILE, TILE), TILE)
        tile_load(i).wait()
        product = dot(act[...], gbuf[lax.rem(i, SLOTS)], 0, 0)
        merged[:, cols] = product + res[:, cols].astype(F32)

        @pl.when(i + SLOTS < n_tiles)
        def _():
            tile_load(i + SLOTS).start()

    def gq_core():
        arrived(lambda: gq.at[:, pl.ds(0, (n_plane - 1) * slice_rows)], 0)
        mine = gq.at[:, pl.ds(pl.multiple_of(core * n_plane * slice_rows, slice_rows), n_plane * slice_rows)]
        remote(mine, mine, 1, partner)

    def left_factor():
        left[dp] = jnp.zeros((rank, rows), F32)

        @pl.loop(0, width // wide)
        def _(i):
            cols = pl.ds(pl.multiple_of(i * wide, wide), wide)
            left[dp] += fold3(dot(query3[:, cols], res[:, cols], 1, 1))

        arrived(lambda: gq.at[:, pl.ds(0, n_plane * slice_rows)], 1)
        step = tokens // 2

        @pl.loop(0, 2)
        def _(i):
            part = pl.ds(pl.multiple_of(i * step, step), step)
            left[dp] += fold3(dot(jnp.concatenate(thirds(gq[:, part]), axis=0), act[part, :], 1, 0))

        to_line("y", lambda dev, _: remote(left.at[dp], left.at[dp], 2, dev))

    def average():
        arrived(lambda: left.at[pl.ds(0, ny - 1)], 2)
        total = left[0]
        for r in range(1, ny):
            total = total + left[r]
        total = total * (1.0 / ny)
        avg[...] = total
        high, low = halves(total)
        avg2[:rank] = high
        avg2[rank:] = low
        gram = dot(total, total, 1, 1, HIGHEST)
        gram_out[...] = jnp.concatenate([gram[:half], gram[half:]], axis=1)
        remote(gram_out, gram_in, 3, partner)

    def gram_sum():
        arrived(lambda: gram_in, 3)
        gram_slots[chip] = gram_out[...] + gram_in[...]
        to_plane("z", "x", lambda dev, _: remote(gram_slots.at[chip], gram_slots.at[chip], 4, dev))

    def right_terms(groups):
        step = 2048

        @pl.loop(groups[0] * gcols // step, (groups[-1] + 1) * gcols // step)
        def _(i):
            cols = pl.ds(pl.multiple_of(i * step, step), step)
            high, low = halves(merged[:, cols])
            both = dot(avg2[...], high, 1, 0)
            tt[:, cols] = both[:rank] + (both[rank:] + dot(avg2[:rank], low, 1, 0))

        theirs = pl.ds(pl.multiple_of(half * (1 - core), half), half)
        for g in groups:
            remote(tt.at[theirs, at_group(g)], core_rx.at[:, at_group(g)], sem_of(g, "core"), partner)

    def line_of(g):
        axis = AXES[g]
        b1, b2 = [a for a in ("y", "z", "x") if a != axis]
        n = sizes[axis]
        n_p = sizes[b1] * sizes[b2]
        return axis, b1, b2, n, half // n, me[b1] * sizes[b2] + me[b2], n_p, gcols // n_p

    def part_rows(p, size):
        return pl.ds(pl.multiple_of(p * size, size), size)

    def core_sum(g):
        cols = at_group(g)
        arrived(lambda: core_rx.at[:, cols], sem_of(g, "core"))
        core_rx[:, cols] = core_rx[:, cols] + tt[part_rows(core, half), cols]
        return cols

    n_col = gcols // 128
    l_group = GROUPS - 1
    l_rows = half * gcols // (128 * n_chips)

    def last_piece(at, top):
        return (pl.ds(pl.multiple_of(top + at // n_col * l_rows, l_rows), l_rows),
                pl.ds(pl.multiple_of(gcols * l_group + at % n_col * 128, 128), 128))

    def last_send():
        core_sum(l_group)
        to_all(lambda dev, p: remote(
            core_rx.at[last_piece(p, 0)], last_rx.at[:, part_rows(place, 128)], sem_of(l_group, "line"), dev))

    def last_gather():
        arrived(lambda: last_rx.at[:, pl.ds(0, (n_chips - 1) * 128)], sem_of(l_group, "line"))
        last_rx[:, part_rows(place, 128)] = core_rx[last_piece(place, 0)]
        total = last_rx[:, 0:128]
        for k in range(1, n_chips):
            total = total + last_rx[:, k * 128:(k + 1) * 128]
        piece = last_piece(place, half * core)
        tf[piece] = total
        to_all(lambda dev, _: remote(tf.at[piece], tf.at[piece], sem_of(l_group, "ag_line"), dev))

    def last_core():
        arrived(lambda: tf.at[pl.ds(0, l_rows), pl.ds(0, (n_chips - 1) * 128)], sem_of(l_group, "ag_line"))
        mine = tf.at[part_rows(core, half), at_group(l_group)]
        remote(mine, mine, sem_of(l_group, "ag_core"), partner)

    def line_send(g):
        axis, _, _, n, lrows, *_ = line_of(g)
        cols = core_sum(g)
        to_line(axis, lambda dev, p: remote(
            core_rx.at[part_rows(p, lrows), cols], line_rx.at[g, part_rows(me[axis], lrows)], sem_of(g, "line"), dev))

    def plane_send(g):
        axis, b1, b2, n, lrows, pos, n_p, pcols = line_of(g)
        arrived(lambda: line_rx.at[g, pl.ds(0, (n - 1) * lrows)], sem_of(g, "line"))
        total = core_rx[part_rows(me[axis], lrows), at_group(g)]
        for k in range(1, n):
            total = total + line_rx[g, part_rows(shift(axis, k), lrows)]
        line_sum[g, :lrows] = total
        to_plane(b1, b2, lambda dev, p: remote(
            line_sum.at[g, pl.ds(0, lrows), part_rows(p, pcols)],
            plane_rx.at[g, pl.ds(0, lrows), part_rows(pos, pcols)], sem_of(g, "plane"), dev))

    def gather_plane(g):
        axis, b1, b2, n, lrows, pos, n_p, pcols = line_of(g)
        rest = pl.ds(0, (n_p - 1) * pcols)
        arrived(lambda: plane_rx.at[g, pl.ds(0, lrows), rest], sem_of(g, "plane"))
        mine = part_rows(pos, pcols)
        plane_rx[g, :lrows, mine] = line_sum[g, :lrows, mine]
        total = plane_rx[g, :lrows, 0:pcols]
        for k in range(1, n_p):
            total = total + plane_rx[g, :lrows, k * pcols:(k + 1) * pcols]
        piece = (pl.ds(pl.multiple_of(half * core + lrows * me[axis], lrows), lrows),
                 pl.ds(pl.multiple_of(gcols * g + pcols * pos, pcols), pcols))
        tf[piece] = total
        to_plane(b1, b2, lambda dev, _: remote(tf.at[piece], tf.at[piece], sem_of(g, "ag_plane"), dev))

    def gather_line(g):
        axis, b1, b2, n, lrows, pos, n_p, pcols = line_of(g)
        arrived(lambda: tf.at[pl.ds(0, lrows), pl.ds(0, (n_p - 1) * pcols)], sem_of(g, "ag_plane"))
        piece = (pl.ds(pl.multiple_of(half * core + lrows * me[axis], lrows), lrows), at_group(g))
        to_line(axis, lambda dev, _: remote(tf.at[piece], tf.at[piece], sem_of(g, "ag_line"), dev))
        remote(tf.at[piece], tf.at[piece], sem_of(g, "ag_core"), partner)

    def gather_core(g):
        axis, b1, b2, n, lrows, *_ = line_of(g)
        arrived(lambda: tf.at[pl.ds(0, (n - 1) * lrows), at_group(g)], sem_of(g, "ag_line"))


        def forward(_, p):
            piece = (pl.ds(pl.multiple_of(half * core + lrows * p, lrows), lrows), at_group(g))
            remote(tf.at[piece], tf.at[piece], sem_of(g, "ag_core"), partner)

        to_line(axis, forward)

    at_row = lax.broadcasted_iota(jnp.int32, (rank, 1), 0)
    at_lane = lax.broadcasted_iota(jnp.int32, (1, 2 * rank), 1)

    def factor_start():
        arrived(lambda: gram_slots.at[pl.ds(0, n_plane - 1)], 4)
        packed = gram_slots[0]
        for k in range(1, n_plane):
            packed = packed + gram_slots[k]
        gram = jnp.concatenate([packed[:, :rank], packed[:, rank:]], axis=0)
        unit = (lax.broadcasted_iota(jnp.int32, (rank, rank), 0) == lax.broadcasted_iota(jnp.int32, (rank, rank), 1)).astype(F32)
        chol[...] = jnp.concatenate([gram, unit], axis=1)

    def factor(start, stop):
        @pl.loop(start, stop)
        def _(k):
            matrix = chol[...]
            row = chol[pl.ds(k, 1), :]
            column = jnp.sum(jnp.where(at_lane == k, matrix, 0.0), axis=1, keepdims=True)
            pivot = jnp.sum(jnp.where(at_lane == k, row, 0.0), axis=1, keepdims=True)
            chol[...] = matrix - jnp.where(at_row > k, column, 0.0) * (row * (1.0 / pivot))

    def factor_end():
        pivots = jnp.sum(jnp.where(at_row == at_lane, chol[...], 0.0), axis=1, keepdims=True)
        inverse = chol[:, rank:] * (1.0 / jnp.sqrt(pivots))
        orth = dot(inverse, avg[...], 1, 0, HIGHEST)
        both = jnp.concatenate([dot(inverse, orth, 0, 0, HIGHEST), inverse.T, jnp.zeros((rank, rank), F32)], axis=1)
        high, low = halves(both * (1.0 / ny))
        wl3[:rank] = high
        wl3[rank:2 * rank] = high
        wl3[2 * rank:] = low

    def finish(g):
        arrived(lambda: tf.at[pl.ds(0, half), at_group(g)], sem_of(g, "ag_core"))
        high, low = halves(tf[:, at_group(g)])
        terms3[:rank, at_group(g)] = high
        terms3[rank:2 * rank, at_group(g)] = low
        terms3[2 * rank:, at_group(g)] = high

    early = list(range(l_group))

    def after_5():
        average()
        right_terms([0])
        right_terms([1])
        line_send(0)
        right_terms([2])
        line_send(1)
        gram_sum()
        line_send(2)

    def after_2():
        gq_core()
        left_factor()

    stages = {2: after_2, 5: after_5}

    @pl.loop(1, n_tiles)
    def _(i):
        tile(i)
        for at, stage in stages.items():
            pl.when(i == at)(stage)

    right_terms([l_group])
    plane_send(0)
    plane_send(1)
    plane_send(2)
    last_send()
    factor_start()
    factor(0, rank // 4)
    gather_plane(0)
    gather_plane(1)
    gather_plane(2)
    last_gather()
    factor(rank // 4, rank // 2)
    gather_line(0)
    gather_line(1)
    gather_line(2)
    factor(rank // 2, rank)
    factor_end()
    gather_core(0)
    gather_core(1)
    gather_core(2)
    last_core()
    finish(0)
    finish(1)
    finish(2)
    finish(l_group)
    for view, sem in sent:
        pltpu.make_async_copy(view(), view(), send.at[sem]).wait()


def write_kernel(merged, terms3, wl3, error_hbm, right_hbm, error, right, sem):
    rows, width = merged.shape
    rank = right.shape[0]

    def copies(i):
        cols = pl.ds(i * TILE, TILE)
        return (pltpu.make_async_copy(error.at[:, cols], error_hbm.at[:, cols], sem.at[0, i]),
                pltpu.make_async_copy(right.at[:, cols], right_hbm.at[:, cols], sem.at[1, i]))

    for i in range(width // TILE):
        cols = pl.ds(i * TILE, TILE)
        both = dot(wl3[:, :rows + rank], terms3[:, cols], 0, 0)
        error[:, cols] = (merged[:, cols] - both[:rows]).astype(BF16)
        right[:, cols] = both[rows:rows + rank]
        for c in copies(i):
            c.start()

    for i in range(width // TILE):
        for c in copies(i):
            c.wait()


def solution(mesh):
    n_dp, n_tp = mesh.shape["dp"], mesh.shape["tp"]
    nx = 4 if n_tp == 32 else 2
    sizes = {"y": n_dp, "z": n_tp // (2 * nx), "x": nx}

    def on_device(activations, out_grads, residual, query_factor):
        tokens, rows = activations.shape
        width, rank = query_factor.shape
        half = rank // 2
        gcols = width // GROUPS
        n_plane = sizes["z"] * sizes["x"]
        lmax = half // min(sizes.values())
        merged, terms3, wl3 = pl.pallas_call(
            functools.partial(kernel, sizes),
            out_shape=(
                pltpu.VMEM((rows, width), F32),
                pltpu.VMEM((3 * rank, width), BF16),
                pltpu.VMEM((3 * rank, rows + 2 * rank), BF16),
            ),
            in_specs=[pl.BlockSpec(memory_space=pl.ANY)] * 4,
            out_specs=(pl.BlockSpec(memory_space=pltpu.VMEM),) * 3,
            scratch_shapes=[
                pltpu.VMEM((tokens, rows), BF16),
                pltpu.VMEM((SLOTS, tokens, TILE), BF16),
                pltpu.VMEM((rows, width), BF16),
                pltpu.VMEM((rank, width), F32),
                pltpu.VMEM((3 * rank, width), BF16),
                pltpu.VMEM((tokens // (2 * n_plane), width), BF16),
                pltpu.VMEM((rank, tokens), F32),
                pltpu.VMEM((n_dp, rank, rows), F32),
                pltpu.VMEM((rank, rows), F32),
                pltpu.VMEM((2 * rank, rows), BF16),
                pltpu.VMEM((half, 2 * rank), F32),
                pltpu.VMEM((half, 2 * rank), F32),
                pltpu.VMEM((n_plane, half, 2 * rank), F32),
                pltpu.VMEM((rank, 2 * rank), F32),
                pltpu.VMEM((rank, width), F32),
                pltpu.VMEM((half, width), F32),
                pltpu.VMEM((GROUPS, half, gcols), F32),
                pltpu.VMEM((GROUPS, lmax, gcols), F32),
                pltpu.VMEM((GROUPS, lmax, gcols), F32),
                pltpu.VMEM((half * gcols // (128 * sizes["y"] * n_plane), sizes["y"] * n_plane * 128), F32),
                pltpu.VMEM((rank, width), F32),
                pltpu.SemaphoreType.DMA((N_SEMS,)),
                pltpu.SemaphoreType.DMA((N_SEMS,)),
                pltpu.SemaphoreType.DMA((4,)),
                pltpu.SemaphoreType.DMA((SLOTS + 2,)),
            ],
            compiler_params=pltpu.CompilerParams(
                collective_id=0, has_side_effects=True, vmem_limit_bytes=50 * 2**20
            ),
            name="powersgd",
        )(activations, out_grads, residual, query_factor.T)
        error, right_t = pl.pallas_call(
            write_kernel,
            out_shape=(jax.ShapeDtypeStruct((rows, width), BF16), jax.ShapeDtypeStruct((rank, width), F32)),
            in_specs=[pl.BlockSpec(memory_space=pltpu.VMEM)] * 3,
            out_specs=(pl.BlockSpec(memory_space=pl.ANY),) * 2,
            scratch_shapes=[
                pltpu.VMEM((rows, width), BF16),
                pltpu.VMEM((rank, width), F32),
                pltpu.SemaphoreType.DMA((2, width // TILE)),
            ],
            compiler_params=pltpu.CompilerParams(vmem_limit_bytes=24 * 2**20),
            name="finish",
        )(*(pltpu.with_memory_space_constraint(v, pltpu.VMEM) for v in (merged, terms3, wl3)))
        return error, right_t.T

    return jax.shard_map(
        on_device,
        mesh=mesh,
        in_specs=(P("dp", "tp"), P("dp", None), P(("dp", "tp"), None), P()),
        out_specs=(P(("dp", "tp"), None), P()),
        check_vma=False,
    )
```
